32 devices in a mesh: groups: 2 (over y), cells: 4 (over z), tm: 4 (over x, core).
Axes of the slice: x: 2, y: 2, z: 4, core: 2. Of those that a mesh axis runs over, the one named last changes fastest.
Arguments:
- observed: float32 [1024, 16384], P('tm', ('groups', 'cells')), parts along dimension 1
- mask: int32 [1024, 16384], P('tm', ('groups', 'cells')), parts along dimension 1, may hold values 0 or 1
- noise: float32 [16384], P(('groups', 'cells')), parts along dimension 0, may hold values from 0.05 to 0.5
- spread: float32 [16384], P(('groups', 'cells')), parts along dimension 0, may hold values from 0.5 to 1
- taps: float32 [32], replicated, may hold values from 0.1 to 1
- neighbours: int32 [8, 16384], P(None, ('groups', 'cells')), parts along dimension 1, may hold values from 0 to 8191, as said below
- regions: int32 [16384], P(('groups', 'cells')), parts along dimension 0, may hold values from 0 to 31, never falling along the last dimension, each value on 1 to 512 neighbouring positions
Outputs:
- solution: float32 [1024, 16384], P('tm', ('groups', 'cells')), parts along dimension 1
- residual: float32 [1024, 16384], P('tm', ('groups', 'cells')), parts along dimension 1
The draws below stay inside these ranges and needn't reach their ends.
There are 2 independent parts, one for each index of `groups`. The reference program is written for one: setup_inputs(seed, part) draws one part's arguments, and reference() takes and returns one part's arrays. A program takes and returns all parts, laid end to end along the dimension named above; an argument that names none is the same for every part. Nothing has to cross between parts.
Inputs may be any that keep to these rules, and one draw needn't show every extreme that they name: For every slot p and cell c, neighbours[p, c] = e implies neighbours[p, e] = c, and |e - c| < 32. `regions`: region ids never fall from one cell to the next.
All inputs are finite; a program needn't handle non-finite values. No bound on the sum of `mask` on one device may be relied on, other than what follows from the above.
Results may differ from the reference program's by a relative error of at most 0.0003.
Values sent between devices are 32-bit elements; how exact they have to be, the bound alone decides.
A program may use at most 192 MiB of HBM per device.

```python
import math
import jax
import jax.numpy as jnp
import numpy as np

W = 32
HB = 32
NBP = 8
RLEN = 256
ITERS = 3
DAYS = 1024
CELLS = 8192
REGIONS = 32


def draw_observed(key, part):
    base = jax.random.normal(key, (DAYS, CELLS), jnp.float32)
    day_pos = jnp.arange(DAYS, dtype=jnp.float32)[:, None] / DAYS
    cell_pos = jnp.arange(CELLS, dtype=jnp.float32)[None, :] / CELLS
    ramp = (1.0 + 2.0 * day_pos) * (1.0 + cell_pos)
    return base * ramp * 0.5


def draw_neighbours(key, part):
    half = HB // 2
    span = HB
    windows = CELLS // span + 2
    cell_ids = jnp.arange(CELLS, dtype=jnp.int32)
    listing = []
    for slot in range(NBP):
        slot_key = jax.random.fold_in(key, 1000 + slot)
        keys = jax.random.split(slot_key, 2)
        offset = jax.random.randint(keys[0], (), 0, span, jnp.int32)
        scores = jax.random.randint(keys[1], (windows, half), 0, 1 << 20, jnp.int32) * half + jnp.arange(half, dtype=jnp.int32)[None, :]
        perm = jnp.argsort(scores, axis=1).astype(jnp.int32)
        inverse = jnp.argsort(perm, axis=1).astype(jnp.int32)
        shifted = cell_ids + offset
        window = shifted // span
        position = shifted % span
        first = position < half
        lower = jnp.minimum(position, half - 1)
        upper = jnp.clip(position - half, 0, half - 1)
        partner_pos = jnp.where(first, half + perm[window, lower], inverse[window, upper])
        partner = cell_ids - position + partner_pos
        valid = (partner >= 0) & (partner < CELLS)
        listing.append(jnp.where(valid, partner, cell_ids).astype(jnp.int32))
    return jnp.stack(listing).astype(jnp.int32)


def plant(entries, rng, smallest, high):
    spot = [jax.random.randint(jax.random.fold_in(rng, axis), (), 0, length) for axis, length in enumerate(entries.shape)]
    widest = entries.shape.index(max(entries.shape))
    next_to = spot[:widest] + [(spot[widest] + 1) % entries.shape[widest]] + spot[widest + 1:]
    return entries.at[tuple(spot)].set(smallest).at[tuple(next_to)].set(high)


def block_scale(key, extent, cuts, smallest, top_value):
    level, own = 1.0, jax.random.fold_in(key, 6)
    for axis_at, parts in cuts:
        heights = jnp.exp(jax.random.uniform(jax.random.fold_in(own, axis_at), (parts,), jnp.float32, smallest / len(cuts), top_value / len(cuts)))
        level = level * jnp.repeat(heights, extent[axis_at] // parts).reshape([-1 if axis == axis_at else 1 for axis in range(len(extent))])
    return level


def split_up(count, total, limit, lean):
    loads = [(1 << 20) // math.isqrt(grade ** lean) + 1 for grade in range(2, count + 1)]
    spare, counts = total - limit - (count - 1), [1] * (count - 1)
    while spare > 0:
        free = [i for i in range(count - 1) if counts[i] < limit]
        whole, remaining = sum([loads[i] for i in free]), spare
        for i in free:
            more = min(limit - counts[i], max(1, remaining * loads[i] // whole), spare)
            counts[i] = counts[i] + more
            spare = spare - more
    return np.array([limit] + counts)


def ragged_sizes(stream_key, number_of, total, limit, slope):
    if number_of == 2:
        one = jax.random.randint(stream_key, (), max(1, total - limit), min(limit, total - 1) + 1)
        return jnp.stack([one, total - one])
    sizes = jnp.asarray(split_up(number_of, total, limit, slope), jnp.int32)
    twos = (number_of - 1) // 2
    donor, taker = sizes[1:1 + 2 * twos:2], sizes[2:2 + 2 * twos:2]
    margin = jnp.minimum(donor - 1, limit - taker)
    moved = jax.random.randint(jax.random.fold_in(stream_key, 1), (twos,), 0, 1 << 20) % (margin + 1)
    sizes = sizes.at[1:1 + 2 * twos:2].set(donor - moved).at[2:2 + 2 * twos:2].set(taker + moved)
    return sizes[jax.random.permutation(jax.random.fold_in(stream_key, 2), number_of)]


def setup_inputs(seed: int = 0, part: int = 0) -> dict:
    seeds = jax.random.split(jax.random.key(seed), 8)
    part_keys = jax.random.split(jax.random.fold_in(seeds[7], part), 8)
    return {
        "observed": draw_observed(jax.random.fold_in(jax.random.fold_in(seeds[7], part), 71), part),
        "mask": plant((jax.random.randint(part_keys[1], (DAYS, CELLS), 0, 4) < 3).astype(jnp.int32), jax.random.fold_in(part_keys[1], 1), 0, 1),
        "noise": jnp.clip(jnp.exp(math.log(0.5) - 2.3025851 * jax.random.uniform(part_keys[2], (CELLS,), jnp.float32) ** block_scale(part_keys[2], (CELLS,), ((0, 4),), -0.2, 0.2)), 0.05, 0.5),
        "spread": jnp.clip(jnp.exp(math.log(1.0) - 0.6931472 * jax.random.uniform(part_keys[3], (CELLS,), jnp.float32) ** block_scale(part_keys[3], (CELLS,), ((0, 4),), -0.2, 0.2)), 0.5, 1.0),
        "taps": jnp.clip(jax.random.uniform(seeds[4], (W,), jnp.float32, 0.1, 1.0), 0.1, 1.0),
        "neighbours": draw_neighbours(jax.random.fold_in(jax.random.fold_in(seeds[7], part), 71), part),
        "regions": jnp.searchsorted(jnp.cumsum(ragged_sizes(part_keys[6], REGIONS, CELLS, 2 * RLEN, 0)), jnp.arange(CELLS), side="right").astype(jnp.int32),
    }


pair_scale = 0.075
temporal_diag = 2.0
tap_total = 0.9


def spatial(values, spread, neighbours, pair_weight):
    scaled = spread[None, :] * values
    mixed = values
    for slot in range(NBP):
        mixed = mixed + pair_weight[slot][None, :] * jnp.take(scaled, neighbours[slot], axis=1)
    return mixed


def temporal(values, coefs):
    smooth = temporal_diag * values
    for offset in range(1, W + 1):
        smooth = smooth + coefs[offset - 1] * (jnp.roll(values, offset, 0) + jnp.roll(values, -offset, 0))
    return smooth


def reference(observed, mask, noise, spread, taps, neighbours, regions):
    maskf = mask.astype(jnp.float32)
    coefs = taps * (tap_total / W)
    same = (jnp.take(regions, neighbours) == regions[None, :]).astype(jnp.float32)
    pair_weight = pair_scale * spread[None, :] * same

    def operate(vector):
        masked = maskf * vector
        return noise[None, :] * vector + maskf * temporal(spatial(masked, spread, neighbours, pair_weight), coefs)

    right = maskf * observed
    solution = jnp.zeros_like(right)
    residual = right
    direction = right
    norm_now = jnp.sum(residual * residual)
    for count in range(ITERS):
        image = operate(direction)
        alpha = norm_now / jnp.sum(direction * image)
        solution = solution + alpha * direction
        residual = residual - alpha * image
        if count + 1 < ITERS:
            norm_next = jnp.sum(residual * residual)
            direction = residual + (norm_next / norm_now) * direction
            norm_now = norm_next
    return solution, residual
```

```python
import functools

import jax
import jax.numpy as jnp
from jax import lax
from jax.experimental import pallas as pl
from jax.experimental.pallas import tpu as pltpu
from jax.sharding import PartitionSpec as P

MESH = pl.DeviceIdType.MESH
W = 32
HB = 32
ITERS = 3
PAIR = 0.075
DIAG = 2.0
TAP_TOTAL = 0.9
SHIFT = 2.3
TAU = 4.0
L = 128
CH = 256
F32 = jnp.float32
BF16 = jnp.bfloat16


def split(values):
    high = values.astype(BF16)
    return high, (values - high.astype(F32)).astype(BF16)


def dot(a, b):
    return jnp.dot(a, b, preferred_element_type=F32)


def combine(factors, vectors):
    total = factors[0] * vectors[0]
    for factor, vector in zip(factors[1:], vectors[1:]):
        total = total + factor * vector
    return total


def polynomial_steps(moments):
    def form(left, right, up):
        total = None
        for i, a in enumerate(left):
            for j, b in enumerate(right):
                term = a * b * moments[i + j + up]
                total = term if total is None else total + term
        return total

    zero = jnp.zeros_like(moments[0])
    residual = [zero + 1.0]
    direction = [zero + 1.0]
    iterate = [zero] * ITERS
    norm_now = moments[0]
    for count in range(ITERS):
        alpha = norm_now / (SHIFT * form(direction, direction, 0) + TAU * form(direction, direction, 1))
        image = [zero] * (len(direction) + 1)
        for k, value in enumerate(direction):
            image[k] = image[k] + SHIFT * value
            image[k + 1] = image[k + 1] + TAU * value
            iterate[k] = iterate[k] + alpha * value
        residual = residual + [zero] * (len(image) - len(residual))
        residual = [r - alpha * q for r, q in zip(residual, image)]
        if count + 1 < ITERS:
            norm_next = form(residual, residual, 0)
            beta = norm_next / norm_now
            padded = direction + [zero] * (len(residual) - len(direction))
            direction = [r + beta * d for r, d in zip(residual, padded)]
            norm_now = norm_next
    return iterate, residual


def kernel(
    n_cells, n_tm,
    taps, observed, mask, noise, spread, neighbours, regions,
    solution_out, residual_out,
    basis, scaled, counts, toeplitz, edge_t, column_ids, region_row, region_send, region_recv,
    day_send, day_recv, cell_send, cell_recv, partial, moments, gather_tm, gather_cells,
    day_ssem, day_rsem, cell_ssem, cell_rsem, region_ssem, region_rsem,
    tm_ssem, tm_rsem, cells_ssem, cells_rsem,
):
    days, tile = observed.shape
    chunks = tile // CH
    slots = neighbours.shape[0]
    my_cells = lax.axis_index("cells")
    my_tm = lax.axis_index("tm")
    after = lax.rem(my_tm + 1, n_tm)
    before = lax.rem(my_tm + n_tm - 1, n_tm)
    has_left = my_cells > 0
    has_right = my_cells < n_cells - 1

    barrier = pltpu.get_barrier_semaphore()
    for step in range(1, n_tm):
        pl.semaphore_signal(
            barrier, inc=1, device_id={"tm": lax.rem(my_tm + step, n_tm)}, device_id_type=MESH
        )
    for step in range(1, n_cells):
        pl.semaphore_signal(
            barrier, inc=1, device_id={"cells": lax.rem(my_cells + step, n_cells)}, device_id_type=MESH
        )
    pl.semaphore_wait(barrier, n_tm + n_cells - 2)

    def to_cells(source, target, ssem, rsem, peer):
        return pltpu.make_async_remote_copy(
            src_ref=source, dst_ref=target, send_sem=ssem, recv_sem=rsem,
            device_id={"cells": peer}, device_id_type=MESH,
        )

    def to_tm(source, target, ssem, rsem, peer):
        return pltpu.make_async_remote_copy(
            src_ref=source, dst_ref=target, send_sem=ssem, recv_sem=rsem,
            device_id={"tm": peer}, device_id_type=MESH,
        )

    def cell_copies(buffer_s, buffer_r, ssem, rsem):
        leftward = to_cells(
            buffer_s.at[0], buffer_r.at[1], ssem.at[0], rsem.at[1], jnp.maximum(my_cells - 1, 0)
        )
        rightward = to_cells(
            buffer_s.at[1], buffer_r.at[0], ssem.at[1], rsem.at[0], jnp.minimum(my_cells + 1, n_cells - 1)
        )
        return leftward, rightward

    def start_cells(copies):
        @pl.when(has_left)
        def _():
            copies[0].start()

        @pl.when(has_right)
        def _():
            copies[1].start()

    def wait_cells(copies):
        @pl.when(has_left)
        def _():
            copies[0].wait_send()
            copies[1].wait_recv()

        @pl.when(has_right)
        def _():
            copies[1].wait_send()
            copies[0].wait_recv()

    region_send[0] = jnp.broadcast_to(regions[:, :L], (8, L))
    region_send[1] = jnp.broadcast_to(regions[:, tile - L :], (8, L))
    region_copies = cell_copies(region_send, region_recv, region_ssem, region_rsem)
    start_cells(region_copies)

    lanes = lax.broadcasted_iota(jnp.int32, (days // 4, L), 1)

    def columns(chunk):
        return pl.ds(pl.multiple_of(chunk * CH, CH), CH)

    def store_scaled(chunk, vector):
        high, low = split(vector * spread[:, columns(chunk)])
        place = pl.ds(pl.multiple_of(L + chunk * CH, L), CH)
        scaled[:days, place] = high
        scaled[days:, place] = low

    def send_edges(level):
        quarter = days // 4
        left = basis[level, :, :L] * spread[:, :L]
        right = basis[level, :, tile - L :] * spread[:, tile - L :]
        for side, block in ((0, left), (1, right)):
            packed = None
            for q in range(4):
                part = block[q * quarter : (q + 1) * quarter]
                shift = (q * HB - (0 if side == 0 else L - HB)) % L
                part = pltpu.roll(part, shift, 1) if shift else part
                packed = part if packed is None else jnp.where(lanes >= q * HB, part, packed)
            cell_send[level, side] = packed
        copies = cell_copies(
            cell_send.at[level], cell_recv.at[level], cell_ssem.at[level], cell_rsem.at[level]
        )
        start_cells(copies)
        return copies

    def take_edges(level, copies):
        quarter = days // 4
        wait_cells(copies)
        for side, flag, base in ((0, has_left, 0), (1, has_right, L + tile)):

            @pl.when(flag)
            def _(side=side, base=base):
                packed = cell_recv[level, side]
                for q in range(4):
                    shift = ((L - HB if side == 0 else 0) - q * HB) % L
                    part = pltpu.roll(packed, shift, 1) if shift else packed
                    keep = lanes >= L - HB if side == 0 else lanes < HB
                    high, low = split(jnp.where(keep, part, 0.0))
                    scaled[q * quarter : (q + 1) * quarter, base : base + L] = high
                    scaled[days + q * quarter : days + (q + 1) * quarter, base : base + L] = low

    scaled[:, :L] = jnp.zeros((2 * days, L), BF16)
    scaled[:, L + tile :] = jnp.zeros((2 * days, L), BF16)

    @pl.loop(0, chunks)
    def _(chunk):
        value = observed[:, columns(chunk)] * mask[:, columns(chunk)].astype(F32)
        basis[0, :, columns(chunk)] = value
        store_scaled(chunk, value)

    copies = send_edges(0)

    region_row[:, L : L + tile] = regions[...]

    def column_block(block):
        row = region_row[:, pl.ds(pl.multiple_of(block * L, L), L)]
        column_ids[pl.ds(pl.multiple_of(block * L, L), L), :] = jnp.broadcast_to(row, (L, L)).T

    @pl.loop(1, 1 + tile // L)
    def _(block):
        column_block(block)

    span = L + 2 * HB
    span_ids = lax.broadcasted_iota(jnp.int32, (span, L), 0)

    def count_chunk(chunk):
        counts[chunk] = jnp.zeros((2 * CH, CH), BF16)
        for half in range(2):
            start = chunk * CH + half * L
            place = pl.ds(pl.multiple_of(start, L), L)
            ids = span_ids + (my_cells * tile + start - HB)
            found = jnp.zeros((span, L), F32)
            for slot in range(slots):
                found = jnp.where(ids == neighbours[pl.ds(slot, 1), place], found + 1.0, found)
            same = column_ids[pl.ds(pl.multiple_of(start + L - HB, HB), span), :] == regions[:, place]
            found = jnp.where(same, found, 0.0)
            counts[chunk, half * L + L - HB : half * L + L - HB + span, half * L : half * L + L] = found.astype(BF16)

    @pl.loop(1, chunks - 1)
    def _(chunk):
        count_chunk(chunk)

    gap = jnp.abs(
        lax.broadcasted_iota(jnp.int32, (days, days), 0) - lax.broadcasted_iota(jnp.int32, (days, days), 1)
    )
    gap_prev = lax.broadcasted_iota(jnp.int32, (W, W), 0) + W - lax.broadcasted_iota(jnp.int32, (W, W), 1)
    gap_next = lax.broadcasted_iota(jnp.int32, (W, W), 1) + W - lax.broadcasted_iota(jnp.int32, (W, W), 0)

    def tap_values(distance):
        def body(k, value):
            return jnp.where(distance == k + 1, taps[k] * (TAP_TOTAL / W / TAU), value)

        return lax.fori_loop(0, W, body, jnp.zeros(distance.shape, F32))

    for row in range(0, days, 64):
        high, low = split(tap_values(gap[row : row + 64]))
        toeplitz[row : row + 64] = high
        toeplitz[days + row : days + row + 64] = low
    for side, distance in ((0, gap_prev), (1, gap_next)):
        high, low = split(tap_values(distance))
        edge_t[side, :W] = high
        edge_t[side, W:] = low

    wait_cells(region_copies)
    region_row[:, :L] = jnp.where(has_left, region_recv[0, :1], -1)
    region_row[:, L + tile :] = jnp.where(has_right, region_recv[1, :1], -1)
    column_block(0)
    column_block(1 + tile // L)
    count_chunk(0)
    count_chunk(chunks - 1)

    moments[...] = jnp.zeros_like(moments)

    def fold(product):
        total = jnp.sum(product.reshape(days // 8, 8, CH), axis=0)
        return total[:, :L] + total[:, L:]

    def day_copies(level, chunk):
        place = columns(chunk)
        return (
            to_tm(
                day_send.at[level, 0, :, place], day_recv.at[level, 1, :, place],
                day_ssem.at[level, 0, chunk], day_rsem.at[level, 1, chunk], before,
            ),
            to_tm(
                day_send.at[level, 1, :, place], day_recv.at[level, 0, :, place],
                day_ssem.at[level, 1, chunk], day_rsem.at[level, 0, chunk], after,
            ),
        )

    def spatial(level, chunk):
        place = columns(chunk)
        window = scaled[:, pl.ds(pl.multiple_of(chunk * CH, CH), 2 * CH)]
        gathered = dot(window, counts[chunk])
        vector = basis[level, :, place]
        mixed = vector + (PAIR * spread[:, place]) * (gathered[:days] + gathered[days:])
        day_send[level, 0, :, place] = mixed[:W]
        day_send[level, 1, :, place] = mixed[days - W :]
        for copy in day_copies(level, chunk):
            copy.start()
        high, low = split(mixed)
        both = dot(toeplitz[...], high)
        smooth = (DIAG / TAU) * mixed + both[:days] + both[days:] + dot(toeplitz[:days], low)
        basis[level + 1, :, place] = smooth

    def finish(level, chunk):
        place = columns(chunk)
        for copy in day_copies(level, chunk):
            copy.wait()
        for side, rows in ((0, slice(0, W)), (1, slice(days - W, days))):
            high, low = split(day_recv[level, side, :, place])
            both = dot(edge_t[side], high)
            basis[level + 1, rows, place] = (
                basis[level + 1, rows, place] + both[:W] + both[W:] + dot(edge_t[side, :W], low)
            )
        vector = basis[level, :, place]
        image = ((noise[:, place] - SHIFT) * (1.0 / TAU)) * vector + mask[:, place].astype(F32) * basis[
            level + 1, :, place
        ]
        basis[level + 1, :, place] = image
        moments[2 * level] += fold(vector * vector)
        moments[2 * level + 1] += fold(vector * image)
        if level + 1 < ITERS:
            store_scaled(chunk, image)

    for level in range(ITERS):

        @pl.loop(1, chunks - 1)
        def _(chunk):
            spatial(level, chunk)

        take_edges(level, copies)

        @pl.loop(0, 2)
        def _(index):
            spatial(level, index * (chunks - 1))

        @pl.loop(1, chunks - 1)
        def _(chunk):
            finish(level, chunk)

        @pl.loop(0, 2)
        def _(index):
            finish(level, index * (chunks - 1))

        if level + 1 < ITERS:
            copies = send_edges(level + 1)

    row_ids = lax.broadcasted_iota(jnp.int32, (8, L), 0)
    packed = jnp.zeros((8, L), F32)
    for k in range(2 * ITERS):
        packed = jnp.where(row_ids == k, jnp.sum(moments[k], axis=0, keepdims=True), packed)
    partial[0] = packed

    def all_sum(source, gathered, ssem, rsem, me, count, send):
        gathered[me] = source[...]
        for step in range(1, count):
            peer = lax.rem(me + step, count)
            send(source, gathered.at[me], ssem.at[step], rsem.at[me], peer).start()
        for step in range(1, count):
            peer = lax.rem(me + step, count)
            send(source, gathered.at[peer], ssem.at[step], rsem.at[peer], peer).wait()
        total = gathered[0]
        for index in range(1, count):
            total = total + gathered[index]
        return total

    partial[1] = all_sum(partial.at[0], gather_tm, tm_ssem, tm_rsem, my_tm, n_tm, to_tm)
    total = all_sum(partial.at[1], gather_cells, cells_ssem, cells_rsem, my_cells, n_cells, to_cells)
    sums = [
        jnp.broadcast_to(jnp.sum(total[k : k + 1], axis=1, keepdims=True), (1, CH)) for k in range(2 * ITERS)
    ]
    iterate, residual = polynomial_steps(sums)

    @pl.loop(0, chunks)
    def _(chunk):
        place = columns(chunk)
        levels = [basis[k, :, place] for k in range(ITERS + 1)]
        solution_out[:, place] = combine(iterate, levels)
        residual_out[:, place] = combine(residual, levels)


def on_device(n_cells, n_tm, observed, mask, noise, spread, taps, neighbours, regions):
    days, tile = observed.shape
    chunks = tile // CH
    dma = pltpu.SemaphoreType.DMA
    vmem = pl.BlockSpec(memory_space=pltpu.VMEM)
    shape = jax.ShapeDtypeStruct(observed.shape, F32)
    return pl.pallas_call(
        functools.partial(kernel, n_cells, n_tm),
        out_shape=(shape, shape),
        in_specs=[pl.BlockSpec(memory_space=pltpu.SMEM)] + [vmem] * 6,
        out_specs=(vmem, vmem),
        scratch_shapes=[
            pltpu.VMEM((ITERS + 1, days, tile), F32),
            pltpu.VMEM((2 * days, tile + 2 * L), BF16),
            pltpu.VMEM((chunks, 2 * CH, CH), BF16),
            pltpu.VMEM((2 * days, days), BF16),
            pltpu.VMEM((2, 2 * W, W), BF16),
            pltpu.VMEM((tile + 2 * L, L), jnp.int32),
            pltpu.VMEM((1, tile + 2 * L), jnp.int32),
            pltpu.VMEM((2, 8, L), jnp.int32),
            pltpu.VMEM((2, 8, L), jnp.int32),
            pltpu.VMEM((ITERS, 2, W, tile), F32),
            pltpu.VMEM((ITERS, 2, W, tile), F32),
            pltpu.VMEM((ITERS, 2, days // 4, L), F32),
            pltpu.VMEM((ITERS, 2, days // 4, L), F32),
            pltpu.VMEM((2, 8, L), F32),
            pltpu.VMEM((2 * ITERS, 8, L), F32),
            pltpu.VMEM((n_tm, 8, L), F32),
            pltpu.VMEM((n_cells, 8, L), F32),
            dma((ITERS, 2, chunks)),
            dma((ITERS, 2, chunks)),
            dma((ITERS, 2)),
            dma((ITERS, 2)),
            dma((2,)),
            dma((2,)),
            dma((n_tm,)),
            dma((n_tm,)),
            dma((n_cells,)),
            dma((n_cells,)),
        ],
        compiler_params=pltpu.CompilerParams(
            collective_id=0, has_side_effects=True, vmem_limit_bytes=56 * 1024 * 1024
        ),
    )(taps, observed, mask, noise[None, :], spread[None, :], neighbours, regions[None, :])


def solution(mesh):
    return jax.shard_map(
        functools.partial(on_device, mesh.shape["cells"], mesh.shape["tm"]),
        mesh=mesh,
        in_specs=(
            P("tm", ("groups", "cells")),
            P("tm", ("groups", "cells")),
            P(("groups", "cells")),
            P(("groups", "cells")),
            P(),
            P(None, ("groups", "cells")),
            P(("groups", "cells")),
        ),
        out_specs=(P("tm", ("groups", "cells")), P("tm", ("groups", "cells"))),
        check_vma=False,
    )
```

```python
import functools

import jax
import jax.numpy as jnp
from jax import lax
from jax.experimental import pallas as pl
from jax.experimental.pallas import tpu as pltpu
from jax.sharding import PartitionSpec as P

MESH = pl.DeviceIdType.MESH
W = 32
HB = 32
ITERS = 3
PAIR = 0.075
DIAG = 2.0
TAP_TOTAL = 0.9
SHIFT = 2.3
TAU = 4.0
L = 128
CH = 256
F32 = jnp.float32
BF16 = jnp.bfloat16


def split(values):
    high = values.astype(BF16)
    return high, (values - high.astype(F32)).astype(BF16)


def dot(a, b):
    return jnp.dot(a, b, preferred_element_type=F32)


def combine(factors, vectors):
    total = factors[0] * vectors[0]
    for factor, vector in zip(factors[1:], vectors[1:]):
        total = total + factor * vector
    return total


def polynomial_steps(moments, rho):
    def form(left, right, up):
        total = None
        for i, a in enumerate(left):
            for j, b in enumerate(right):
                term = a * b * moments[i + j + up]
                total = term if total is None else total + term
        return total

    zero = jnp.zeros_like(moments[0])
    residual = [zero + 1.0]
    direction = [zero + 1.0]
    iterate = [zero] * ITERS
    norm_now = moments[0]
    for count in range(ITERS):
        alpha = norm_now / (rho * form(direction, direction, 0) + TAU * form(direction, direction, 1))
        image = [zero] * (len(direction) + 1)
        for k, value in enumerate(direction):
            image[k] = image[k] + rho * value
            image[k + 1] = image[k + 1] + TAU * value
            iterate[k] = iterate[k] + alpha * value
        residual = residual + [zero] * (len(image) - len(residual))
        residual = [r - alpha * q for r, q in zip(residual, image)]
        if count + 1 < ITERS:
            norm_next = form(residual, residual, 0)
            beta = norm_next / norm_now
            padded = direction + [zero] * (len(residual) - len(direction))
            direction = [r + beta * d for r, d in zip(residual, padded)]
            norm_now = norm_next
    return iterate, residual


def kernel(
    n_cells, n_tm,
    taps, observed_hbm, mask_hbm, noise, spread, neighbours, regions,
    basis_out, factors_out,
    observed, mask, basis, scaled, counts, toeplitz, edge_t, column_ids, region_row, region_send, region_recv,
    day_send, day_recv, cell_send, cell_recv, partial, moments, gather_tm, gather_cells, lead,
    day_ssem, day_rsem, cell_ssem, cell_rsem, region_ssem, region_rsem,
    tm_ssem, tm_rsem, cells_ssem, cells_rsem, load_sem, store_sem,
):
    days, tile = observed.shape
    chunks = tile // CH
    slots = neighbours.shape[0]
    my_cells = lax.axis_index("cells")
    my_tm = lax.axis_index("tm")
    after = lax.rem(my_tm + 1, n_tm)
    before = lax.rem(my_tm + n_tm - 1, n_tm)
    has_left = my_cells > 0
    has_right = my_cells < n_cells - 1

    barrier = pltpu.get_barrier_semaphore()
    for step in range(1, n_tm):
        pl.semaphore_signal(
            barrier, inc=1, device_id={"tm": lax.rem(my_tm + step, n_tm)}, device_id_type=MESH
        )
    for step in range(1, n_cells):
        pl.semaphore_signal(
            barrier, inc=1, device_id={"cells": lax.rem(my_cells + step, n_cells)}, device_id_type=MESH
        )
    loads = (
        pltpu.make_async_copy(observed_hbm, observed, load_sem.at[0]),
        pltpu.make_async_copy(mask_hbm, mask, load_sem.at[1]),
    )
    for load in loads:
        load.start()

    def to_cells(source, target, ssem, rsem, peer):
        return pltpu.make_async_remote_copy(
            src_ref=source, dst_ref=target, send_sem=ssem, recv_sem=rsem,
            device_id={"cells": peer}, device_id_type=MESH,
        )

    def to_tm(source, target, ssem, rsem, peer):
        return pltpu.make_async_remote_copy(
            src_ref=source, dst_ref=target, send_sem=ssem, recv_sem=rsem,
            device_id={"tm": peer}, device_id_type=MESH,
        )

    def cell_copies(buffer_s, buffer_r, ssem, rsem):
        leftward = to_cells(
            buffer_s.at[0], buffer_r.at[1], ssem.at[0], rsem.at[1], jnp.maximum(my_cells - 1, 0)
        )
        rightward = to_cells(
            buffer_s.at[1], buffer_r.at[0], ssem.at[1], rsem.at[0], jnp.minimum(my_cells + 1, n_cells - 1)
        )
        return leftward, rightward

    def start_cells(copies):
        @pl.when(has_left)
        def _():
            copies[0].start()

        @pl.when(has_right)
        def _():
            copies[1].start()

    def wait_cells(copies):
        @pl.when(has_left)
        def _():
            copies[0].wait_send()
            copies[1].wait_recv()

        @pl.when(has_right)
        def _():
            copies[1].wait_send()
            copies[0].wait_recv()

    lanes = lax.broadcasted_iota(jnp.int32, (days // 4, L), 1)

    def columns(chunk):
        return pl.ds(pl.multiple_of(chunk * CH, CH), CH)

    def store_scaled(chunk, vector):
        high, low = split(vector * spread[:, columns(chunk)])
        place = pl.ds(pl.multiple_of(L + chunk * CH, L), CH)
        scaled[:days, place] = high
        scaled[days:, place] = low

    def send_edges(level):
        quarter = days // 4
        left = basis[level, :, :L] * spread[:, :L]
        right = basis[level, :, tile - L :] * spread[:, tile - L :]
        for side, block in ((0, left), (1, right)):
            packed = None
            for q in range(4):
                part = block[q * quarter : (q + 1) * quarter]
                shift = (q * HB - (0 if side == 0 else L - HB)) % L
                part = pltpu.roll(part, shift, 1) if shift else part
                packed = part if packed is None else jnp.where(lanes >= q * HB, part, packed)
            cell_send[level, side] = packed
        copies = cell_copies(
            cell_send.at[level], cell_recv.at[level], cell_ssem.at[level], cell_rsem.at[level]
        )
        start_cells(copies)
        return copies

    def take_edges(level, copies):
        quarter = days // 4
        wait_cells(copies)
        for side, flag, base in ((0, has_left, 0), (1, has_right, L + tile)):

            @pl.when(flag)
            def _(side=side, base=base):
                packed = cell_recv[level, side]
                for q in range(4):
                    shift = ((L - HB if side == 0 else 0) - q * HB) % L
                    part = pltpu.roll(packed, shift, 1) if shift else packed
                    keep = lanes >= L - HB if side == 0 else lanes < HB
                    high, low = split(jnp.where(keep, part, 0.0))
                    scaled[q * quarter : (q + 1) * quarter, base : base + L] = high
                    scaled[days + q * quarter : days + (q + 1) * quarter, base : base + L] = low

    region_row[:, L : L + tile] = regions[...]

    def column_block(block):
        row = region_row[:, pl.ds(pl.multiple_of(block * L, L), L)]
        column_ids[pl.ds(pl.multiple_of(block * L, L), L), :] = jnp.broadcast_to(row, (L, L)).T

    span = L + 2 * HB
    span_ids = lax.broadcasted_iota(jnp.int32, (span, L), 0)

    def count_chunk(chunk):
        counts[chunk] = jnp.zeros((2 * CH, CH), BF16)
        for half in range(2):
            start = chunk * CH + half * L
            place = pl.ds(pl.multiple_of(start, L), L)
            ids = span_ids + (my_cells * tile + start - HB)
            found = jnp.zeros((span, L), F32)
            for slot in range(slots):
                found = jnp.where(ids == neighbours[pl.ds(slot, 1), place], found + 1.0, found)
            same = column_ids[pl.ds(pl.multiple_of(start + L - HB, HB), span), :] == regions[:, place]
            found = jnp.where(same, found, 0.0)
            counts[chunk, half * L + L - HB : half * L + L - HB + span, half * L : half * L + L] = found.astype(BF16)

    gap = jnp.abs(
        lax.broadcasted_iota(jnp.int32, (days, days), 0) - lax.broadcasted_iota(jnp.int32, (days, days), 1)
    )
    gap_prev = lax.broadcasted_iota(jnp.int32, (W, W), 0) + W - lax.broadcasted_iota(jnp.int32, (W, W), 1)
    gap_next = lax.broadcasted_iota(jnp.int32, (W, W), 1) + W - lax.broadcasted_iota(jnp.int32, (W, W), 0)

    def tap_values(distance):
        def body(k, value):
            return jnp.where(distance == k + 1, taps[k] * (TAP_TOTAL / W / TAU), value)

        return lax.fori_loop(0, W, body, jnp.zeros(distance.shape, F32))

    for row in range(0, days, 64):
        high, low = split(tap_values(gap[row : row + 64]))
        toeplitz[row : row + 64] = high
        toeplitz[days + row : days + row + 64] = low
    for side, distance in ((0, gap_prev), (1, gap_next)):
        high, low = split(tap_values(distance))
        edge_t[side, :W] = high
        edge_t[side, W:] = low

    @pl.loop(1, 1 + tile // L)
    def _(block):
        column_block(block)

    pl.semaphore_wait(barrier, n_tm + n_cells - 2)

    region_send[0] = jnp.broadcast_to(regions[:, :L], (8, L))
    region_send[1] = jnp.broadcast_to(regions[:, tile - L :], (8, L))
    region_copies = cell_copies(region_send, region_recv, region_ssem, region_rsem)
    start_cells(region_copies)

    scaled[:, :L] = jnp.zeros((2 * days, L), BF16)
    scaled[:, L + tile :] = jnp.zeros((2 * days, L), BF16)

    for load in loads:
        load.wait()

    @pl.loop(0, chunks)
    def _(chunk):
        value = observed[:, columns(chunk)] * mask[:, columns(chunk)].astype(F32)
        basis[0, :, columns(chunk)] = value
        store_scaled(chunk, value)

    copies = send_edges(0)

    moments[...] = jnp.zeros_like(moments)

    def fold(product):
        total = jnp.sum(product.reshape(days // 8, 8, CH), axis=0)
        return total[:, :L] + total[:, L:]

    def day_copies(level, chunk):
        place = columns(chunk)
        return (
            to_tm(
                day_send.at[level, 0, :, place], day_recv.at[level, 1, :, place],
                day_ssem.at[level, 0, chunk], day_rsem.at[level, 1, chunk], before,
            ),
            to_tm(
                day_send.at[level, 1, :, place], day_recv.at[level, 0, :, place],
                day_ssem.at[level, 1, chunk], day_rsem.at[level, 0, chunk], after,
            ),
        )

    def spatial(level, chunk):
        place = columns(chunk)
        window = scaled[:, pl.ds(pl.multiple_of(chunk * CH, CH), 2 * CH)]
        gathered = dot(window, counts[chunk])
        vector = basis[level, :, place]
        mixed = vector + (PAIR * spread[:, place]) * (gathered[:days] + gathered[days:])
        day_send[level, 0, :, place] = mixed[:W]
        day_send[level, 1, :, place] = mixed[days - W :]
        for copy in day_copies(level, chunk):
            copy.start()
        high, low = split(mixed)
        both = dot(toeplitz[...], high)
        smooth = (DIAG / TAU) * mixed + both[:days] + both[days:] + dot(toeplitz[:days], low)
        basis[level + 1, :, place] = smooth

    def finish(level, chunk):
        place = columns(chunk)
        for copy in day_copies(level, chunk):
            copy.wait()
        for side, rows in ((0, slice(0, W)), (1, slice(days - W, days))):
            high, low = split(day_recv[level, side, :, place])
            both = dot(edge_t[side], high)
            basis[level + 1, rows, place] = (
                basis[level + 1, rows, place] + both[:W] + both[W:] + dot(edge_t[side, :W], low)
            )
        vector = basis[level, :, place]
        image = ((noise[:, place] - SHIFT) * (1.0 / TAU)) * vector + mask[:, place].astype(F32) * basis[
            level + 1, :, place
        ]
        if level == 1:
            start = basis[0, :, place]
            other = vector - lead[:, :CH] * start
            image = image - lead[:, :CH] * (vector + other)
            vector = other
            basis[1, :, place] = vector
        elif level == 2:
            image = image - lead[:, :CH] * vector
        basis[level + 1, :, place] = image
        moments[2 * level] += fold(vector * vector)
        moments[2 * level + 1] += fold(vector * image)
        if level + 1 < ITERS:
            store_scaled(chunk, image)

    row_ids = lax.broadcasted_iota(jnp.int32, (8, L), 0)

    def start_sum(source, gathered, ssem, rsem, me, count, send):
        gathered[me] = source[...]
        for step in range(1, count):
            peer = lax.rem(me + step, count)
            send(source, gathered.at[me], ssem.at[step], rsem.at[me], peer).start()

    def end_sum(source, gathered, ssem, rsem, me, count, send):
        for step in range(1, count):
            peer = lax.rem(me + step, count)
            send(source, gathered.at[peer], ssem.at[step], rsem.at[peer], peer).wait()
        total = gathered[0]
        for index in range(1, count):
            total = total + gathered[index]
        return total

    def over_tm(turn):
        return (partial.at[turn, 0], gather_tm.at[turn], tm_ssem.at[turn], tm_rsem.at[turn], my_tm, n_tm, to_tm)

    def over_cells(turn):
        return (
            partial.at[turn, 1], gather_cells.at[turn], cells_ssem.at[turn], cells_rsem.at[turn],
            my_cells, n_cells, to_cells,
        )

    def sums_begin(turn, first, last):
        packed = jnp.zeros((8, L), F32)
        for k in range(first, last):
            packed = jnp.where(row_ids == k, jnp.sum(moments[k], axis=0, keepdims=True), packed)
        partial[turn, 0] = packed
        start_sum(*over_tm(turn))

    def sums_middle(turn):
        partial[turn, 1] = end_sum(*over_tm(turn))
        start_sum(*over_cells(turn))

    def sums_end(turn, first, last):
        total = end_sum(*over_cells(turn))
        return [
            jnp.broadcast_to(jnp.sum(total[k : k + 1], axis=1, keepdims=True), (1, CH))
            for k in range(first, last)
        ]

    def save(level):
        return pltpu.make_async_copy(basis.at[level], basis_out.at[level], store_sem.at[level])

    last = chunks - 1
    outer = (1, last - 1, 0, last)
    inner = [c for k in range(2, chunks // 2) for c in (k, last - k)]

    for chunk in outer[:2]:
        count_chunk(chunk)
        spatial(0, chunk)
    wait_cells(region_copies)
    region_row[:, :L] = jnp.where(has_left, region_recv[0, :1], -1)
    region_row[:, L + tile :] = jnp.where(has_right, region_recv[1, :1], -1)
    column_block(0)
    column_block(1 + tile // L)
    take_edges(0, copies)
    for chunk in outer[2:]:
        count_chunk(chunk)
        spatial(0, chunk)
    for chunk in inner:
        count_chunk(chunk)
        spatial(0, chunk)

    factor_now = None
    for level in range(ITERS - 1):
        if level == 1:
            sums = sums_end(0, 0, 2)
            factor_now = sums[1] / sums[0]
            lead[...] = factor_now
            norm_first = sums[0]
        for chunk in outer:
            finish(level, chunk)
        copies = send_edges(level + 1)
        for low, high in ((2, 1), (last - 2, last - 1)):
            finish(level, low)
            spatial(level + 1, high)
        take_edges(level + 1, copies)
        spatial(level + 1, 0)
        spatial(level + 1, last)
        rest = inner[2:]
        for chunk in rest:
            finish(level, chunk)
        save(level).start()
        if level == 0:
            sums_begin(0, 0, 2)
        half = len(inner) // 2
        for chunk in inner[:half]:
            spatial(level + 1, chunk)
        if level == 0:
            sums_middle(0)
        for chunk in inner[half:]:
            spatial(level + 1, chunk)
    save(ITERS - 1).start()
    for chunk in outer:
        finish(ITERS - 1, chunk)
    for chunk in inner:
        finish(ITERS - 1, chunk)
    save(ITERS).start()
    sums_begin(1, 2, 2 * ITERS)
    sums_middle(1)
    rho = SHIFT + TAU * factor_now
    tail = sums_end(1, 2, 2 * ITERS)
    iterate, residual = polynomial_steps([norm_first, jnp.zeros_like(norm_first)] + tail, rho)
    for k, value in enumerate(iterate + residual):
        factors_out[pl.ds(k, 1), :] = value[:, :L]
    factors_out[pl.ds(2 * ITERS + 1, 1), :] = jnp.zeros((1, L), F32)
    for level in range(ITERS + 1):
        save(level).wait()


def combine_kernel(factors, basis, solution_out, residual_out):
    levels = [basis[k] for k in range(ITERS + 1)]
    solution_out[...] = combine([factors[k, 0] for k in range(ITERS)], levels)
    residual_out[...] = combine([factors[k, 0] for k in range(ITERS, 2 * ITERS + 1)], levels)


def on_device(n_cells, n_tm, observed, mask, noise, spread, taps, neighbours, regions):
    days, tile = observed.shape
    chunks = tile // CH
    dma = pltpu.SemaphoreType.DMA
    vmem = pl.BlockSpec(memory_space=pltpu.VMEM)
    shape = jax.ShapeDtypeStruct(observed.shape, F32)
    basis, factors = pl.pallas_call(
        functools.partial(kernel, n_cells, n_tm),
        out_shape=(
            jax.ShapeDtypeStruct((ITERS + 1, days, tile), F32),
            jax.ShapeDtypeStruct((8, L), F32),
        ),
        in_specs=[pl.BlockSpec(memory_space=pltpu.SMEM)] + [pl.BlockSpec(memory_space=pl.ANY)] * 2 + [vmem] * 4,
        out_specs=(pl.BlockSpec(memory_space=pl.ANY), vmem),
        scratch_shapes=[
            pltpu.VMEM((days, tile), F32),
            pltpu.VMEM((days, tile), jnp.int32),
            pltpu.VMEM((ITERS + 1, days, tile), F32),
            pltpu.VMEM((2 * days, tile + 2 * L), BF16),
            pltpu.VMEM((chunks, 2 * CH, CH), BF16),
            pltpu.VMEM((2 * days, days), BF16),
            pltpu.VMEM((2, 2 * W, W), BF16),
            pltpu.VMEM((tile + 2 * L, L), jnp.int32),
            pltpu.VMEM((1, tile + 2 * L), jnp.int32),
            pltpu.VMEM((2, 8, L), jnp.int32),
            pltpu.VMEM((2, 8, L), jnp.int32),
            pltpu.VMEM((ITERS, 2, W, tile), F32),
            pltpu.VMEM((ITERS, 2, W, tile), F32),
            pltpu.VMEM((ITERS, 2, days // 4, L), F32),
            pltpu.VMEM((ITERS, 2, days // 4, L), F32),
            pltpu.VMEM((2, 2, 8, L), F32),
            pltpu.VMEM((2 * ITERS, 8, L), F32),
            pltpu.VMEM((2, n_tm, 8, L), F32),
            pltpu.VMEM((2, n_cells, 8, L), F32),
            pltpu.VMEM((1, CH), F32),
            dma((ITERS, 2, chunks)),
            dma((ITERS, 2, chunks)),
            dma((ITERS, 2)),
            dma((ITERS, 2)),
            dma((2,)),
            dma((2,)),
            dma((2, n_tm)),
            dma((2, n_tm)),
            dma((2, n_cells)),
            dma((2, n_cells)),
            dma((2,)),
            dma((ITERS + 1,)),
        ],
        compiler_params=pltpu.CompilerParams(
            collective_id=0, has_side_effects=True, vmem_limit_bytes=56 * 1024 * 1024
        ),
    )(taps, observed, mask, noise[None, :], spread[None, :], neighbours, regions[None, :])
    rows = 32
    block = pl.BlockSpec((rows, tile), lambda i: (i, 0))
    return pl.pallas_call(
        combine_kernel,
        grid=(days // rows,),
        out_shape=(shape, shape),
        in_specs=[
            pl.BlockSpec(memory_space=pltpu.SMEM),
            pl.BlockSpec((ITERS + 1, rows, tile), lambda i: (0, i, 0)),
        ],
        out_specs=(block, block),
    )(factors, basis)


def solution(mesh):
    return jax.shard_map(
        functools.partial(on_device, mesh.shape["cells"], mesh.shape["tm"]),
        mesh=mesh,
        in_specs=(
            P("tm", ("groups", "cells")),
            P("tm", ("groups", "cells")),
            P(("groups", "cells")),
            P(("groups", "cells")),
            P(),
            P(None, ("groups", "cells")),
            P(("groups", "cells")),
        ),
        out_specs=(P("tm", ("groups", "cells")), P("tm", ("groups", "cells"))),
        check_vma=False,
    )
```

```python
import functools

import jax
import jax.numpy as jnp
from jax import lax
from jax.experimental import pallas as pl
from jax.experimental.pallas import tpu as pltpu
from jax.sharding import PartitionSpec as P

MESH = pl.DeviceIdType.MESH
W = 32
HB = 32
ITERS = 3
PAIR = 0.075
DIAG = 2.0
TAP_TOTAL = 0.9
SHIFT = 2.3
TAU = 4.0
L = 128
CH = 256
F32 = jnp.float32
BF16 = jnp.bfloat16


def split(values):
    high = values.astype(BF16)
    return high, (values - high.astype(F32)).astype(BF16)


def dot(a, b):
    return jnp.dot(a, b, preferred_element_type=F32)


def combine(factors, vectors):
    total = factors[0] * vectors[0]
    for factor, vector in zip(factors[1:], vectors[1:]):
        total = total + factor * vector
    return total


def polynomial_steps(moments, rho):
    def form(left, right, up):
        total = None
        for i, a in enumerate(left):
            for j, b in enumerate(right):
                term = a * b * moments[i + j + up]
                total = term if total is None else total + term
        return total

    zero = jnp.zeros_like(moments[0])
    residual = [zero + 1.0]
    direction = [zero + 1.0]
    iterate = [zero] * ITERS
    norm_now = moments[0]
    for count in range(ITERS):
        alpha = norm_now / (rho * form(direction, direction, 0) + TAU * form(direction, direction, 1))
        image = [zero] * (len(direction) + 1)
        for k, value in enumerate(direction):
            image[k] = image[k] + rho * value
            image[k + 1] = image[k + 1] + TAU * value
            iterate[k] = iterate[k] + alpha * value
        residual = residual + [zero] * (len(image) - len(residual))
        residual = [r - alpha * q for r, q in zip(residual, image)]
        if count + 1 < ITERS:
            norm_next = form(residual, residual, 0)
            beta = norm_next / norm_now
            padded = direction + [zero] * (len(residual) - len(direction))
            direction = [r + beta * d for r, d in zip(residual, padded)]
            norm_now = norm_next
    return iterate, residual


def kernel(
    n_cells, n_tm,
    taps, observed_hbm, mask_hbm, noise, spread, neighbours, regions,
    basis_out, factors_out,
    observed, mask, basis, scaled, counts, toeplitz, edge_t, column_ids, region_row, region_send, region_recv,
    day_send, day_recv, cell_send, cell_recv, partial, moments, gather_tm, gather_cells, lead,
    day_ssem, day_rsem, cell_ssem, cell_rsem, region_ssem, region_rsem,
    tm_ssem, tm_rsem, cells_ssem, cells_rsem, load_sem, store_sem,
):
    days, tile = observed.shape
    chunks = tile // CH
    slots = neighbours.shape[0]
    my_cells = lax.axis_index("cells")
    my_tm = lax.axis_index("tm")
    after = lax.rem(my_tm + 1, n_tm)
    before = lax.rem(my_tm + n_tm - 1, n_tm)
    has_left = my_cells > 0
    has_right = my_cells < n_cells - 1

    barrier = pltpu.get_barrier_semaphore()
    for step in range(1, n_tm):
        pl.semaphore_signal(
            barrier, inc=1, device_id={"tm": lax.rem(my_tm + step, n_tm)}, device_id_type=MESH
        )
    for step in range(1, n_cells):
        pl.semaphore_signal(
            barrier, inc=1, device_id={"cells": lax.rem(my_cells + step, n_cells)}, device_id_type=MESH
        )
    loads = (
        pltpu.make_async_copy(observed_hbm, observed, load_sem.at[0]),
        pltpu.make_async_copy(mask_hbm, mask, load_sem.at[1]),
    )
    for load in loads:
        load.start()

    def to_cells(source, target, ssem, rsem, peer):
        return pltpu.make_async_remote_copy(
            src_ref=source, dst_ref=target, send_sem=ssem, recv_sem=rsem,
            device_id={"cells": peer}, device_id_type=MESH,
        )

    def to_tm(source, target, ssem, rsem, peer):
        return pltpu.make_async_remote_copy(
            src_ref=source, dst_ref=target, send_sem=ssem, recv_sem=rsem,
            device_id={"tm": peer}, device_id_type=MESH,
        )

    def cell_copies(buffer_s, buffer_r, ssem, rsem):
        leftward = to_cells(
            buffer_s.at[0], buffer_r.at[1], ssem.at[0], rsem.at[1], jnp.maximum(my_cells - 1, 0)
        )
        rightward = to_cells(
            buffer_s.at[1], buffer_r.at[0], ssem.at[1], rsem.at[0], jnp.minimum(my_cells + 1, n_cells - 1)
        )
        return leftward, rightward

    def start_cells(copies):
        @pl.when(has_left)
        def _():
            copies[0].start()

        @pl.when(has_right)
        def _():
            copies[1].start()

    def wait_cells(copies):
        @pl.when(has_left)
        def _():
            copies[0].wait_send()
            copies[1].wait_recv()

        @pl.when(has_right)
        def _():
            copies[1].wait_send()
            copies[0].wait_recv()

    lanes = lax.broadcasted_iota(jnp.int32, (days // 4, L), 1)

    def columns(chunk):
        return pl.ds(chunk * CH if isinstance(chunk, int) else pl.multiple_of(chunk * CH, CH), CH)

    def store_scaled(chunk, vector):
        high, low = split(vector * spread[:, columns(chunk)])
        start = L + chunk * CH
        place = pl.ds(start if isinstance(chunk, int) else pl.multiple_of(start, L), CH)
        scaled[:days, place] = high
        scaled[days:, place] = low

    def send_edges(level):
        quarter = days // 4
        left = basis[level, :, :L] * spread[:, :L]
        right = basis[level, :, tile - L :] * spread[:, tile - L :]
        for side, block in ((0, left), (1, right)):
            packed = None
            for q in range(4):
                part = block[q * quarter : (q + 1) * quarter]
                shift = (q * HB - (0 if side == 0 else L - HB)) % L
                part = pltpu.roll(part, shift, 1) if shift else part
                packed = part if packed is None else jnp.where(lanes >= q * HB, part, packed)
            cell_send[level, side] = packed
        copies = cell_copies(
            cell_send.at[level], cell_recv.at[level], cell_ssem.at[level], cell_rsem.at[level]
        )
        start_cells(copies)
        return copies

    def take_edges(level, copies):
        quarter = days // 4
        wait_cells(copies)
        for side, flag, base in ((0, has_left, 0), (1, has_right, L + tile)):

            @pl.when(flag)
            def _(side=side, base=base):
                packed = cell_recv[level, side]
                for q in range(4):
                    shift = ((L - HB if side == 0 else 0) - q * HB) % L
                    part = pltpu.roll(packed, shift, 1) if shift else packed
                    keep = lanes >= L - HB if side == 0 else lanes < HB
                    high, low = split(jnp.where(keep, part, 0.0))
                    scaled[q * quarter : (q + 1) * quarter, base : base + L] = high
                    scaled[days + q * quarter : days + (q + 1) * quarter, base : base + L] = low

    region_row[:, L : L + tile] = regions[...]

    eye = lax.broadcasted_iota(jnp.int32, (L, L), 0) == lax.broadcasted_iota(jnp.int32, (L, L), 1)
    ones = jnp.ones((L, L), BF16)

    def column_block(block):
        row = region_row[:, block * L : (block + 1) * L].astype(F32)
        diagonal = jnp.where(eye, row, 0.0).astype(BF16)
        column_ids[block * L : (block + 1) * L, :] = dot(diagonal, ones)

    span = L + 2 * HB
    span_ids = lax.broadcasted_iota(jnp.int32, (span, L), 0)

    def count_chunk(chunk):
        counts[chunk] = jnp.zeros((2 * CH, CH), BF16)
        for half in range(2):
            start = chunk * CH + half * L
            place = pl.ds(start, L)
            ids = span_ids + (my_cells * tile + start - HB)
            found = jnp.zeros((span, L), F32)
            for slot in range(slots):
                found = jnp.where(ids == neighbours[pl.ds(slot, 1), place], found + 1.0, found)
            same = column_ids[start + L - HB : start + L - HB + span, :] == regions[:, place].astype(F32)
            found = jnp.where(same, found, 0.0)
            counts[chunk, half * L + L - HB : half * L + L - HB + span, half * L : half * L + L] = found.astype(BF16)

    rows_t = 2 * W
    gap = jnp.abs(
        lax.broadcasted_iota(jnp.int32, (rows_t, L), 0) + W - lax.broadcasted_iota(jnp.int32, (rows_t, L), 1)
    )
    band = jnp.zeros((rows_t, L), F32)
    for k in range(W):
        band = jnp.where(gap == k + 1, taps[k] * (TAP_TOTAL / W / TAU), band)
    wide = jnp.concatenate([band, jnp.zeros((rows_t, days - L), F32)], axis=1)
    lanes_t = lax.broadcasted_iota(jnp.int32, (rows_t, days), 1)
    for row in range(0, days, rows_t):
        shift = (row - W) % days
        near = pltpu.roll(wide, shift, 1) if shift else wide
        near = jnp.where((lanes_t >= row - W) & (lanes_t < row + rows_t + W), near, 0.0)
        high, low = split(near)
        toeplitz[row : row + rows_t] = jnp.concatenate([high, low, high], axis=1)
    for side, part in ((0, band[:W, :W]), (1, band[W:, L - W :])):
        high, low = split(part)
        edge_t[side] = jnp.concatenate([high, low, high], axis=1)

    for block in range(1, 1 + tile // L):
        column_block(block)

    pl.semaphore_wait(barrier, n_tm + n_cells - 2)

    region_send[0] = jnp.broadcast_to(regions[:, :L], (8, L))
    region_send[1] = jnp.broadcast_to(regions[:, tile - L :], (8, L))
    region_copies = cell_copies(region_send, region_recv, region_ssem, region_rsem)
    start_cells(region_copies)

    scaled[:, :L] = jnp.zeros((2 * days, L), BF16)
    scaled[:, L + tile :] = jnp.zeros((2 * days, L), BF16)

    for load in loads:
        load.wait()

    @pl.loop(0, chunks)
    def _(chunk):
        value = observed[:, columns(chunk)] * mask[:, columns(chunk)].astype(F32)
        basis[0, :, columns(chunk)] = value
        store_scaled(chunk, value)

    copies = send_edges(0)

    moments[...] = jnp.zeros_like(moments)

    def fold(product):
        total = jnp.sum(product.reshape(days // 8, 8, CH), axis=0)
        return total[:, :L] + total[:, L:]

    def day_copies(level, group):
        place = pl.ds(group * 2 * CH, 2 * CH)
        return (
            to_tm(
                day_send.at[level, 0, :, place], day_recv.at[level, 1, :, place],
                day_ssem.at[level, 0, group], day_rsem.at[level, 1, group], before,
            ),
            to_tm(
                day_send.at[level, 1, :, place], day_recv.at[level, 0, :, place],
                day_ssem.at[level, 1, group], day_rsem.at[level, 0, group], after,
            ),
        )

    def gather(level, chunk):
        place = columns(chunk)
        window = pl.ds(chunk * CH, 2 * CH)
        both = jnp.concatenate([scaled[:days, window], scaled[days:, window]], axis=1)
        gathered = dot(both, jnp.concatenate([counts[chunk], counts[chunk]], axis=0))
        mixed = basis[level, :, place] + (PAIR * spread[:, place]) * gathered
        day_send[level, 0, :, place] = mixed[:W]
        day_send[level, 1, :, place] = mixed[days - W :]
        basis[level + 1, :, place] = mixed

    def smoothen(level, chunk):
        place = columns(chunk)
        mixed = basis[level + 1, :, place]
        high, low = split(mixed)
        basis[level + 1, :, place] = (DIAG / TAU) * mixed + dot(
            toeplitz[...], jnp.concatenate([high, high, low], axis=0)
        )

    def spatial(level, pair):
        for group in pair:
            for chunk in (2 * group, 2 * group + 1):
                gather(level, chunk)
        for group in pair:
            for copy in day_copies(level, group):
                copy.start()
        for group in pair:
            for chunk in (2 * group, 2 * group + 1):
                smoothen(level, chunk)

    def finish(level, pair):
        for group in pair:
            for copy in day_copies(level, group):
                copy.wait()
        for group in pair:
            for chunk in (2 * group, 2 * group + 1):
                finish_chunk(level, chunk)

    def finish_chunk(level, chunk):
        place = columns(chunk)
        smooth = basis[level + 1, :, place]
        ends = []
        for side in range(2):
            high, low = split(day_recv[level, side, :, place])
            ends.append(dot(edge_t[side], jnp.concatenate([high, high, low], axis=0)))
        smooth = jnp.concatenate(
            [smooth[:W] + ends[0], smooth[W : days - W], smooth[days - W :] + ends[1]], axis=0
        )
        vector = basis[level, :, place]
        image = ((noise[:, place] - SHIFT) * (1.0 / TAU)) * vector + mask[:, place].astype(F32) * smooth
        if level == 1:
            start = basis[0, :, place]
            other = vector - lead[:, :CH] * start
            image = image - lead[:, :CH] * (vector + other)
            vector = other
            basis[1, :, place] = vector
        elif level == 2:
            image = image - lead[:, :CH] * vector
        basis[level + 1, :, place] = image
        moments[2 * level] += fold(vector * vector)
        moments[2 * level + 1] += fold(vector * image)
        if level + 1 < ITERS:
            store_scaled(chunk, image)

    row_ids = lax.broadcasted_iota(jnp.int32, (8, L), 0)

    def start_sum(source, gathered, ssem, rsem, me, count, send):
        gathered[me] = source[...]
        for step in range(1, count):
            peer = lax.rem(me + step, count)
            send(source, gathered.at[me], ssem.at[step], rsem.at[me], peer).start()

    def end_sum(source, gathered, ssem, rsem, me, count, send):
        for step in range(1, count):
            peer = lax.rem(me + step, count)
            send(source, gathered.at[peer], ssem.at[step], rsem.at[peer], peer).wait()
        total = gathered[0]
        for index in range(1, count):
            total = total + gathered[index]
        return total

    def over_tm(turn):
        return (partial.at[turn, 0], gather_tm.at[turn], tm_ssem.at[turn], tm_rsem.at[turn], my_tm, n_tm, to_tm)

    def over_cells(turn):
        return (
            partial.at[turn, 1], gather_cells.at[turn], cells_ssem.at[turn], cells_rsem.at[turn],
            my_cells, n_cells, to_cells,
        )

    def sums_begin(turn, first, last):
        packed = jnp.zeros((8, L), F32)
        for k in range(first, last):
            packed = jnp.where(row_ids == k, jnp.sum(moments[k], axis=0, keepdims=True), packed)
        partial[turn, 0] = packed
        start_sum(*over_tm(turn))

    def sums_middle(turn):
        partial[turn, 1] = end_sum(*over_tm(turn))
        start_sum(*over_cells(turn))

    def sums_end(turn, first, last):
        total = end_sum(*over_cells(turn))
        return [
            jnp.broadcast_to(jnp.sum(total[k : k + 1], axis=1, keepdims=True), (1, CH))
            for k in range(first, last)
        ]

    def save(level):
        return pltpu.make_async_copy(basis.at[level], basis_out.at[level], store_sem.at[level])

    groups = chunks // 2
    inner = tuple(range(1, groups - 1))
    outer = (0, groups - 1)

    for group in inner:
        count_chunk(2 * group)
        count_chunk(2 * group + 1)
    spatial(0, inner)
    wait_cells(region_copies)
    region_row[:, :L] = jnp.where(has_left, region_recv[0, :1], -1)
    region_row[:, L + tile :] = jnp.where(has_right, region_recv[1, :1], -1)
    column_block(0)
    column_block(1 + tile // L)
    for group in outer:
        count_chunk(2 * group)
        count_chunk(2 * group + 1)
    take_edges(0, copies)
    spatial(0, outer)

    for level in range(ITERS - 1):
        if level == 1:
            sums = sums_end(0, 0, 2)
            factor_now = sums[1] / sums[0]
            lead[...] = factor_now
            norm_first = sums[0]
        finish(level, inner)
        finish(level, outer)
        copies = send_edges(level + 1)
        save(level).start()
        if level == 0:
            sums_begin(0, 0, 2)
        spatial(level + 1, inner)
        if level == 0:
            sums_middle(0)
        take_edges(level + 1, copies)
        spatial(level + 1, outer)
    save(ITERS - 1).start()
    finish(ITERS - 1, inner)
    finish(ITERS - 1, outer)
    save(ITERS).start()
    sums_begin(1, 2, 2 * ITERS)
    sums_middle(1)
    rho = SHIFT + TAU * factor_now
    tail = sums_end(1, 2, 2 * ITERS)
    iterate, residual = polynomial_steps([norm_first, jnp.zeros_like(norm_first)] + tail, rho)
    for k, value in enumerate(iterate + residual):
        factors_out[pl.ds(k, 1), :] = value[:, :L]
    factors_out[pl.ds(2 * ITERS + 1, 1), :] = jnp.zeros((1, L), F32)
    for level in range(ITERS + 1):
        save(level).wait()


def combine_kernel(factors, basis, solution_out, residual_out):
    levels = [basis[k] for k in range(ITERS + 1)]
    solution_out[...] = combine([factors[k, 0] for k in range(ITERS)], levels)
    residual_out[...] = combine([factors[k, 0] for k in range(ITERS, 2 * ITERS + 1)], levels)


def on_device(n_cells, n_tm, observed, mask, noise, spread, taps, neighbours, regions):
    days, tile = observed.shape
    chunks = tile // CH
    dma = pltpu.SemaphoreType.DMA
    vmem = pl.BlockSpec(memory_space=pltpu.VMEM)
    shape = jax.ShapeDtypeStruct(observed.shape, F32)
    basis, factors = pl.pallas_call(
        functools.partial(kernel, n_cells, n_tm),
        out_shape=(
            pltpu.VMEM((ITERS + 1, days, tile), F32),
            jax.ShapeDtypeStruct((8, L), F32),
        ),
        in_specs=[pl.BlockSpec(memory_space=pltpu.SMEM)] + [pl.BlockSpec(memory_space=pl.ANY)] * 2 + [vmem] * 4,
        out_specs=(pl.BlockSpec(memory_space=pl.ANY), vmem),
        scratch_shapes=[
            pltpu.VMEM((days, tile), F32),
            pltpu.VMEM((days, tile), jnp.int32),
            pltpu.VMEM((ITERS + 1, days, tile), F32),
            pltpu.VMEM((2 * days, tile + 2 * L), BF16),
            pltpu.VMEM((chunks, 2 * CH, CH), BF16),
            pltpu.VMEM((days, 3 * days), BF16),
            pltpu.VMEM((2, W, 3 * W), BF16),
            pltpu.VMEM((tile + 2 * L, L), F32),
            pltpu.VMEM((1, tile + 2 * L), jnp.int32),
            pltpu.VMEM((2, 8, L), jnp.int32),
            pltpu.VMEM((2, 8, L), jnp.int32),
            pltpu.VMEM((ITERS, 2, W, tile), F32),
            pltpu.VMEM((ITERS, 2, W, tile), F32),
            pltpu.VMEM((ITERS, 2, days // 4, L), F32),
            pltpu.VMEM((ITERS, 2, days // 4, L), F32),
            pltpu.VMEM((2, 2, 8, L), F32),
            pltpu.VMEM((2 * ITERS, 8, L), F32),
            pltpu.VMEM((2, n_tm, 8, L), F32),
            pltpu.VMEM((2, n_cells, 8, L), F32),
            pltpu.VMEM((1, CH), F32),
            dma((ITERS, 2, chunks // 2)),
            dma((ITERS, 2, chunks // 2)),
            dma((ITERS, 2)),
            dma((ITERS, 2)),
            dma((2,)),
            dma((2,)),
            dma((2, n_tm)),
            dma((2, n_tm)),
            dma((2, n_cells)),
            dma((2, n_cells)),
            dma((2,)),
            dma((ITERS + 1,)),
        ],
        compiler_params=pltpu.CompilerParams(
            collective_id=0, has_side_effects=True, vmem_limit_bytes=36 * 1024 * 1024
        ),
    )(taps, observed, mask, noise[None, :], spread[None, :], neighbours, regions[None, :])
    rows = 32
    block = pl.BlockSpec((rows, tile), lambda i: (i, 0))
    return pl.pallas_call(
        combine_kernel,
        grid=(days // rows,),
        out_shape=(shape, shape),
        in_specs=[
            pl.BlockSpec(memory_space=pltpu.SMEM),
            pl.BlockSpec((ITERS + 1, rows, tile), lambda i: (0, i, 0)),
        ],
        out_specs=(block, block),
    )(factors, basis)


def solution(mesh):
    return jax.shard_map(
        functools.partial(on_device, mesh.shape["cells"], mesh.shape["tm"]),
        mesh=mesh,
        in_specs=(
            P("tm", ("groups", "cells")),
            P("tm", ("groups", "cells")),
            P(("groups", "cells")),
            P(("groups", "cells")),
            P(),
            P(None, ("groups", "cells")),
            P(("groups", "cells")),
        ),
        out_specs=(P("tm", ("groups", "cells")), P("tm", ("groups", "cells"))),
        check_vma=False,
    )
```

```python
import functools

import jax
import jax.numpy as jnp
from jax import lax
from jax.experimental import pallas as pl
from jax.experimental.pallas import tpu as pltpu
from jax.sharding import PartitionSpec as P

MESH = pl.DeviceIdType.MESH
W = 32
HB = 32
ITERS = 3
PAIR = 0.075
DIAG = 2.0
TAP_TOTAL = 0.9
SHIFT = 2.3
TAU = 4.0
L = 128
CH = 256
F32 = jnp.float32
BF16 = jnp.bfloat16


def split(values):
    high = values.astype(BF16)
    return high, (values - high.astype(F32)).astype(BF16)


def dot(a, b):
    return jnp.dot(a, b, preferred_element_type=F32)


def combine(factors, vectors):
    total = factors[0] * vectors[0]
    for factor, vector in zip(factors[1:], vectors[1:]):
        total = total + factor * vector
    return total


def polynomial_steps(moments, rho):
    def form(left, right, up):
        total = None
        for i, a in enumerate(left):
            for j, b in enumerate(right):
                term = a * b * moments[i + j + up]
                total = term if total is None else total + term
        return total

    zero = jnp.zeros_like(moments[0])
    residual = [zero + 1.0]
    direction = [zero + 1.0]
    iterate = [zero] * ITERS
    norm_now = moments[0]
    for count in range(ITERS):
        alpha = norm_now / (rho * form(direction, direction, 0) + TAU * form(direction, direction, 1))
        image = [zero] * (len(direction) + 1)
        for k, value in enumerate(direction):
            image[k] = image[k] + rho * value
            image[k + 1] = image[k + 1] + TAU * value
            iterate[k] = iterate[k] + alpha * value
        residual = residual + [zero] * (len(image) - len(residual))
        residual = [r - alpha * q for r, q in zip(residual, image)]
        if count + 1 < ITERS:
            norm_next = form(residual, residual, 0)
            beta = norm_next / norm_now
            padded = direction + [zero] * (len(residual) - len(direction))
            direction = [r + beta * d for r, d in zip(residual, padded)]
            norm_now = norm_next
    return iterate, residual


def kernel(
    n_cells, n_tm,
    taps, observed_hbm, mask_hbm, noise, spread, neighbours, regions,
    solution_out, residual_out,
    observed, mask, last_residual, basis, scaled, counts, toeplitz, edge_t, column_ids, region_row, region_send, region_recv,
    day_send, day_recv, cell_send, cell_recv, partial, moments, gather_tm, gather_cells, lead,
    day_ssem, day_rsem, cell_ssem, cell_rsem, region_ssem, region_rsem,
    tm_ssem, tm_rsem, cells_ssem, cells_rsem, load_sem, store_sem,
):
    days, tile = observed.shape
    chunks = tile // CH
    slots = neighbours.shape[0]
    my_cells = lax.axis_index("cells")
    my_tm = lax.axis_index("tm")
    after = lax.rem(my_tm + 1, n_tm)
    before = lax.rem(my_tm + n_tm - 1, n_tm)
    has_left = my_cells > 0
    has_right = my_cells < n_cells - 1

    barrier = pltpu.get_barrier_semaphore()
    for step in range(1, n_tm):
        pl.semaphore_signal(
            barrier, inc=1, device_id={"tm": lax.rem(my_tm + step, n_tm)}, device_id_type=MESH
        )
    for step in range(1, n_cells):
        pl.semaphore_signal(
            barrier, inc=1, device_id={"cells": lax.rem(my_cells + step, n_cells)}, device_id_type=MESH
        )
    groups = tile // (2 * CH)

    def loads(group):
        place = pl.ds(group * 2 * CH, 2 * CH)
        return (
            pltpu.make_async_copy(observed_hbm.at[:, place], observed.at[:, place], load_sem.at[0, group]),
            pltpu.make_async_copy(mask_hbm.at[:, place], mask.at[:, place], load_sem.at[1, group]),
        )

    order = (0, groups - 1) + tuple(range(1, groups - 1))
    for group in order:
        for load in loads(group):
            load.start()

    def to_cells(source, target, ssem, rsem, peer):
        return pltpu.make_async_remote_copy(
            src_ref=source, dst_ref=target, send_sem=ssem, recv_sem=rsem,
            device_id={"cells": peer}, device_id_type=MESH,
        )

    def to_tm(source, target, ssem, rsem, peer):
        return pltpu.make_async_remote_copy(
            src_ref=source, dst_ref=target, send_sem=ssem, recv_sem=rsem,
            device_id={"tm": peer}, device_id_type=MESH,
        )

    def cell_copies(buffer_s, buffer_r, ssem, rsem):
        leftward = to_cells(
            buffer_s.at[0], buffer_r.at[1], ssem.at[0], rsem.at[1], jnp.maximum(my_cells - 1, 0)
        )
        rightward = to_cells(
            buffer_s.at[1], buffer_r.at[0], ssem.at[1], rsem.at[0], jnp.minimum(my_cells + 1, n_cells - 1)
        )
        return leftward, rightward

    def start_cells(copies):
        @pl.when(has_left)
        def _():
            copies[0].start()

        @pl.when(has_right)
        def _():
            copies[1].start()

    def wait_cells(copies):
        @pl.when(has_left)
        def _():
            copies[0].wait_send()
            copies[1].wait_recv()

        @pl.when(has_right)
        def _():
            copies[1].wait_send()
            copies[0].wait_recv()

    lanes = lax.broadcasted_iota(jnp.int32, (days // 4, L), 1)

    def columns(chunk):
        return pl.ds(chunk * CH if isinstance(chunk, int) else pl.multiple_of(chunk * CH, CH), CH)

    def store_scaled(chunk, vector):
        high, low = split(vector * spread[:, columns(chunk)])
        start = L + chunk * CH
        place = pl.ds(start if isinstance(chunk, int) else pl.multiple_of(start, L), CH)
        scaled[:days, place] = high
        scaled[days:, place] = low

    def send_edges(level):
        quarter = days // 4
        left = basis[level, :, :L] * spread[:, :L]
        right = basis[level, :, tile - L :] * spread[:, tile - L :]
        for side, block in ((0, left), (1, right)):
            packed = None
            for q in range(4):
                part = block[q * quarter : (q + 1) * quarter]
                shift = (q * HB - (0 if side == 0 else L - HB)) % L
                part = pltpu.roll(part, shift, 1) if shift else part
                packed = part if packed is None else jnp.where(lanes >= q * HB, part, packed)
            cell_send[level, side] = packed
        copies = cell_copies(
            cell_send.at[level], cell_recv.at[level], cell_ssem.at[level], cell_rsem.at[level]
        )
        start_cells(copies)
        return copies

    def take_edges(level, copies):
        quarter = days // 4
        wait_cells(copies)
        for side, flag, base in ((0, has_left, 0), (1, has_right, L + tile)):

            @pl.when(flag)
            def _(side=side, base=base):
                packed = cell_recv[level, side]
                for q in range(4):
                    shift = ((L - HB if side == 0 else 0) - q * HB) % L
                    part = pltpu.roll(packed, shift, 1) if shift else packed
                    keep = lanes >= L - HB if side == 0 else lanes < HB
                    high, low = split(jnp.where(keep, part, 0.0))
                    scaled[q * quarter : (q + 1) * quarter, base : base + L] = high
                    scaled[days + q * quarter : days + (q + 1) * quarter, base : base + L] = low

    region_row[:, L : L + tile] = regions[...]

    eye = lax.broadcasted_iota(jnp.int32, (L, L), 0) == lax.broadcasted_iota(jnp.int32, (L, L), 1)
    ones = jnp.ones((L, L), BF16)

    def column_block(block):
        row = region_row[:, block * L : (block + 1) * L].astype(F32)
        diagonal = jnp.where(eye, row, 0.0).astype(BF16)
        column_ids[block * L : (block + 1) * L, :] = dot(diagonal, ones)

    span = L + 2 * HB
    span_ids = lax.broadcasted_iota(jnp.int32, (span, L), 0)

    def count_chunk(chunk):
        counts[chunk] = jnp.zeros((2 * CH, CH), BF16)
        for half in range(2):
            start = chunk * CH + half * L
            place = pl.ds(start, L)
            ids = span_ids + (my_cells * tile + start - HB)
            found = jnp.zeros((span, L), F32)
            for slot in range(slots):
                found = jnp.where(ids == neighbours[pl.ds(slot, 1), place], found + 1.0, found)
            same = column_ids[start + L - HB : start + L - HB + span, :] == regions[:, place].astype(F32)
            found = jnp.where(same, found, 0.0)
            counts[chunk, half * L + L - HB : half * L + L - HB + span, half * L : half * L + L] = found.astype(BF16)

    rows_t = 2 * W
    gap = jnp.abs(
        lax.broadcasted_iota(jnp.int32, (rows_t, L), 0) + W - lax.broadcasted_iota(jnp.int32, (rows_t, L), 1)
    )
    band = jnp.zeros((rows_t, L), F32)
    for k in range(W):
        band = jnp.where(gap == k + 1, taps[k] * (TAP_TOTAL / W / TAU), band)
    wide = jnp.concatenate([band, jnp.zeros((rows_t, days - L), F32)], axis=1)
    lanes_t = lax.broadcasted_iota(jnp.int32, (rows_t, days), 1)
    for row in range(0, days, rows_t):
        shift = (row - W) % days
        near = pltpu.roll(wide, shift, 1) if shift else wide
        near = jnp.where((lanes_t >= row - W) & (lanes_t < row + rows_t + W), near, 0.0)
        high, low = split(near)
        toeplitz[row : row + rows_t] = jnp.concatenate([high, low, high], axis=1)
    for side, part in ((0, band[:W, :W]), (1, band[W:, L - W :])):
        high, low = split(part)
        edge_t[side] = jnp.concatenate([high, low, high], axis=1)

    for block in range(1, 1 + tile // L):
        column_block(block)

    pl.semaphore_wait(barrier, n_tm + n_cells - 2)

    region_send[0] = jnp.broadcast_to(regions[:, :L], (8, L))
    region_send[1] = jnp.broadcast_to(regions[:, tile - L :], (8, L))
    region_copies = cell_copies(region_send, region_recv, region_ssem, region_rsem)
    start_cells(region_copies)

    scaled[:, :L] = jnp.zeros((2 * days, L), BF16)
    scaled[:, L + tile :] = jnp.zeros((2 * days, L), BF16)

    def first_vector(group):
        for load in loads(group):
            load.wait()
        for chunk in (2 * group, 2 * group + 1):
            value = observed[:, columns(chunk)] * mask[:, columns(chunk)].astype(F32)
            basis[0, :, columns(chunk)] = value
            store_scaled(chunk, value)

    first_vector(0)
    first_vector(groups - 1)
    copies = send_edges(0)
    for group in order[2:]:
        first_vector(group)

    moments[...] = jnp.zeros_like(moments)

    def fold(product):
        total = jnp.sum(product.reshape(days // 8, 8, CH), axis=0)
        return total[:, :L] + total[:, L:]

    def day_copies(level, run):
        place = pl.ds(run[0] * CH, len(run) * CH)
        return (
            to_tm(
                day_send.at[level, 0, :, place], day_recv.at[level, 1, :, place],
                day_ssem.at[level, 0, run[0]], day_rsem.at[level, 1, run[0]], before,
            ),
            to_tm(
                day_send.at[level, 1, :, place], day_recv.at[level, 0, :, place],
                day_ssem.at[level, 1, run[0]], day_rsem.at[level, 0, run[0]], after,
            ),
        )

    def gather(level, chunk):
        place = columns(chunk)
        window = pl.ds(chunk * CH, 2 * CH)
        both = jnp.concatenate([scaled[:days, window], scaled[days:, window]], axis=1)
        gathered = dot(both, jnp.concatenate([counts[chunk], counts[chunk]], axis=0))
        mixed = basis[level, :, place] + (PAIR * spread[:, place]) * gathered
        day_send[level, 0, :, place] = mixed[:W]
        day_send[level, 1, :, place] = mixed[days - W :]
        basis[level + 1, :, place] = mixed

    def smoothen(level, chunk):
        place = columns(chunk)
        mixed = basis[level + 1, :, place]
        high, low = split(mixed)
        basis[level + 1, :, place] = (DIAG / TAU) * mixed + dot(
            toeplitz[...], jnp.concatenate([high, high, low], axis=0)
        )

    def spatial(level, runs):
        for run in runs:
            for chunk in run:
                gather(level, chunk)
        for run in runs:
            for copy in day_copies(level, run):
                copy.start()
        for run in runs:
            for chunk in run:
                smoothen(level, chunk)

    def finish(level, runs):
        for run in runs:
            for copy in day_copies(level, run):
                copy.wait()
        for run in runs:
            for chunk in run:
                finish_chunk(level, chunk)

    def finish_chunk(level, chunk):
        place = columns(chunk)
        smooth = basis[level + 1, :, place]
        ends = []
        for side in range(2):
            high, low = split(day_recv[level, side, :, place])
            ends.append(dot(edge_t[side], jnp.concatenate([high, high, low], axis=0)))
        smooth = jnp.concatenate(
            [smooth[:W] + ends[0], smooth[W : days - W], smooth[days - W :] + ends[1]], axis=0
        )
        vector = basis[level, :, place]
        image = ((noise[:, place] - SHIFT) * (1.0 / TAU)) * vector + mask[:, place].astype(F32) * smooth
        if level == 1:
            start = basis[0, :, place]
            other = vector - lead[:, :CH] * start
            image = image - lead[:, :CH] * (vector + other)
            vector = other
            basis[1, :, place] = vector
        elif level == 2:
            image = image - lead[:, :CH] * vector
        basis[level + 1, :, place] = image
        moments[2 * level] += fold(vector * vector)
        moments[2 * level + 1] += fold(vector * image)
        if level + 1 < ITERS:
            store_scaled(chunk, image)

    row_ids = lax.broadcasted_iota(jnp.int32, (8, L), 0)

    def start_sum(source, gathered, ssem, rsem, me, count, send):
        gathered[me] = source[...]
        for step in range(1, count):
            peer = lax.rem(me + step, count)
            send(source, gathered.at[me], ssem.at[step], rsem.at[me], peer).start()

    def end_sum(source, gathered, ssem, rsem, me, count, send):
        for step in range(1, count):
            peer = lax.rem(me + step, count)
            send(source, gathered.at[peer], ssem.at[step], rsem.at[peer], peer).wait()
        total = gathered[0]
        for index in range(1, count):
            total = total + gathered[index]
        return total

    def over_tm(turn):
        return (partial.at[turn, 0], gather_tm.at[turn], tm_ssem.at[turn], tm_rsem.at[turn], my_tm, n_tm, to_tm)

    def over_cells(turn):
        return (
            partial.at[turn, 1], gather_cells.at[turn], cells_ssem.at[turn], cells_rsem.at[turn],
            my_cells, n_cells, to_cells,
        )

    def sums_begin(turn, first, last):
        packed = jnp.zeros((8, L), F32)
        for k in range(first, last):
            packed = jnp.where(row_ids == k, jnp.sum(moments[k], axis=0, keepdims=True), packed)
        partial[turn, 0] = packed
        start_sum(*over_tm(turn))

    def sums_middle(turn):
        partial[turn, 1] = end_sum(*over_tm(turn))
        start_sum(*over_cells(turn))

    def sums_end(turn, first, last):
        total = end_sum(*over_cells(turn))
        return [
            jnp.broadcast_to(jnp.sum(total[k : k + 1], axis=1, keepdims=True), (1, CH))
            for k in range(first, last)
        ]

    half = chunks // 2
    middle = ((half - 1, half),)
    rest = (tuple(range(1, half - 1)), tuple(range(half + 1, chunks - 1)))
    ends = ((0,), (chunks - 1,))

    def count_runs(runs):
        for run in runs:
            for chunk in run:
                count_chunk(chunk)

    count_runs(middle)
    spatial(0, middle)
    count_runs(rest)
    spatial(0, rest)
    wait_cells(region_copies)
    region_row[:, :L] = jnp.where(has_left, region_recv[0, :1], -1)
    region_row[:, L + tile :] = jnp.where(has_right, region_recv[1, :1], -1)
    column_block(0)
    column_block(1 + tile // L)
    count_runs(ends)
    take_edges(0, copies)
    spatial(0, ends)

    for level in range(ITERS - 1):
        if level == 1:
            sums = sums_end(0, 0, 2)
            factor_now = sums[1] / sums[0]
            lead[...] = factor_now
            norm_first = sums[0]
        finish(level, middle)
        finish(level, rest)
        spatial(level + 1, middle)
        finish(level, ends)
        copies = send_edges(level + 1)
        if level == 0:
            sums_begin(0, 0, 2)
        spatial(level + 1, rest)
        if level == 0:
            sums_middle(0)
        take_edges(level + 1, copies)
        spatial(level + 1, ends)
    finish(ITERS - 1, middle)
    finish(ITERS - 1, rest)
    finish(ITERS - 1, ends)
    sums_begin(1, 2, 2 * ITERS)
    sums_middle(1)
    rho = SHIFT + TAU * factor_now
    tail = sums_end(1, 2, 2 * ITERS)
    iterate, residual = polynomial_steps([norm_first, jnp.zeros_like(norm_first)] + tail, rho)

    def save(group):
        place = pl.ds(group * 2 * CH, 2 * CH)
        return (
            pltpu.make_async_copy(observed.at[:, place], solution_out.at[:, place], store_sem.at[0, group]),
            pltpu.make_async_copy(last_residual.at[:, place], residual_out.at[:, place], store_sem.at[1, group]),
        )

    for group in range(groups):
        for chunk in (2 * group, 2 * group + 1):
            place = columns(chunk)
            levels = [basis[k, :, place] for k in range(ITERS + 1)]
            observed[:, place] = combine(iterate, levels)
            last_residual[:, place] = combine(residual, levels)
        for copy in save(group):
            copy.start()
    for group in range(groups):
        for copy in save(group):
            copy.wait()


def on_device(n_cells, n_tm, observed, mask, noise, spread, taps, neighbours, regions):
    days, tile = observed.shape
    chunks = tile // CH
    dma = pltpu.SemaphoreType.DMA
    vmem = pl.BlockSpec(memory_space=pltpu.VMEM)
    return pl.pallas_call(
        functools.partial(kernel, n_cells, n_tm),
        out_shape=(pltpu.VMEM((days, tile), F32), pltpu.VMEM((days, tile), F32)),
        in_specs=[pl.BlockSpec(memory_space=pltpu.SMEM)] + [pl.BlockSpec(memory_space=pl.ANY)] * 2 + [vmem] * 4,
        out_specs=(pl.BlockSpec(memory_space=pl.ANY), pl.BlockSpec(memory_space=pl.ANY)),
        scratch_shapes=[
            pltpu.VMEM((days, tile), F32),
            pltpu.VMEM((days, tile), jnp.int32),
            pltpu.VMEM((days, tile), F32),
            pltpu.VMEM((ITERS + 1, days, tile), F32),
            pltpu.VMEM((2 * days, tile + 2 * L), BF16),
            pltpu.VMEM((chunks, 2 * CH, CH), BF16),
            pltpu.VMEM((days, 3 * days), BF16),
            pltpu.VMEM((2, W, 3 * W), BF16),
            pltpu.VMEM((tile + 2 * L, L), F32),
            pltpu.VMEM((1, tile + 2 * L), jnp.int32),
            pltpu.VMEM((2, 8, L), jnp.int32),
            pltpu.VMEM((2, 8, L), jnp.int32),
            pltpu.VMEM((ITERS, 2, W, tile), F32),
            pltpu.VMEM((ITERS, 2, W, tile), F32),
            pltpu.VMEM((ITERS, 2, days // 4, L), F32),
            pltpu.VMEM((ITERS, 2, days // 4, L), F32),
            pltpu.VMEM((2, 2, 8, L), F32),
            pltpu.VMEM((2 * ITERS, 8, L), F32),
            pltpu.VMEM((2, n_tm, 8, L), F32),
            pltpu.VMEM((2, n_cells, 8, L), F32),
            pltpu.VMEM((1, CH), F32),
            dma((ITERS, 2, chunks)),
            dma((ITERS, 2, chunks)),
            dma((ITERS, 2)),
            dma((ITERS, 2)),
            dma((2,)),
            dma((2,)),
            dma((2, n_tm)),
            dma((2, n_tm)),
            dma((2, n_cells)),
            dma((2, n_cells)),
            dma((2, chunks // 2)),
            dma((2, chunks // 2)),
        ],
        compiler_params=pltpu.CompilerParams(
            collective_id=0, has_side_effects=True, vmem_limit_bytes=52 * 1024 * 1024
        ),
    )(taps, observed, mask, noise[None, :], spread[None, :], neighbours, regions[None, :])


def solution(mesh):
    return jax.shard_map(
        functools.partial(on_device, mesh.shape["cells"], mesh.shape["tm"]),
        mesh=mesh,
        in_specs=(
            P("tm", ("groups", "cells")),
            P("tm", ("groups", "cells")),
            P(("groups", "cells")),
            P(("groups", "cells")),
            P(),
            P(None, ("groups", "cells")),
            P(("groups", "cells")),
        ),
        out_specs=(P("tm", ("groups", "cells")), P("tm", ("groups", "cells"))),
        check_vma=False,
    )
```

```python
import functools

import jax
import jax.numpy as jnp
from jax import lax
from jax.experimental import pallas as pl
from jax.experimental.pallas import tpu as pltpu
from jax.sharding import PartitionSpec as P

MESH = pl.DeviceIdType.MESH
W = 32
HB = 32
ITERS = 3
PAIR = 0.075
DIAG = 2.0
TAP_TOTAL = 0.9
SHIFT = 2.3
TAU = 4.0
L = 128
CH = 256
F32 = jnp.float32
BF16 = jnp.bfloat16


def split(values):
    high = values.astype(BF16)
    return high, (values - high.astype(F32)).astype(BF16)


def dot(a, b):
    return jnp.dot(a, b, preferred_element_type=F32)


def combine(factors, vectors):
    total = factors[0] * vectors[0]
    for factor, vector in zip(factors[1:], vectors[1:]):
        total = total + factor * vector
    return total


def polynomial_steps(moments, rho):
    def form(left, right, up):
        total = None
        for i, a in enumerate(left):
            for j, b in enumerate(right):
                term = a * b * moments[i + j + up]
                total = term if total is None else total + term
        return total

    zero = jnp.zeros_like(moments[0])
    residual = [zero + 1.0]
    direction = [zero + 1.0]
    iterate = [zero] * ITERS
    norm_now = moments[0]
    for count in range(ITERS):
        alpha = norm_now / (rho * form(direction, direction, 0) + TAU * form(direction, direction, 1))
        image = [zero] * (len(direction) + 1)
        for k, value in enumerate(direction):
            image[k] = image[k] + rho * value
            image[k + 1] = image[k + 1] + TAU * value
            iterate[k] = iterate[k] + alpha * value
        residual = residual + [zero] * (len(image) - len(residual))
        residual = [r - alpha * q for r, q in zip(residual, image)]
        if count + 1 < ITERS:
            norm_next = form(residual, residual, 0)
            beta = norm_next / norm_now
            padded = direction + [zero] * (len(residual) - len(direction))
            direction = [r + beta * d for r, d in zip(residual, padded)]
            norm_now = norm_next
    return iterate, residual


def kernel(
    n_cells, n_tm,
    taps, observed_hbm, mask_hbm, noise, spread, neighbours, regions,
    solution_out, residual_out,
    observed, mask, last_residual, basis, scaled, counts, toeplitz, edge_t, column_ids, region_row, region_send, region_recv,
    day_send, day_recv, cell_send, cell_recv, partial, moments, gather_tm, gather_cells, lead,
    day_ssem, day_rsem, cell_ssem, cell_rsem, region_ssem, region_rsem,
    tm_ssem, tm_rsem, cells_ssem, cells_rsem, load_sem, store_sem, gather_all, all_ssem, all_rsem,
):
    days, tile = observed.shape
    chunks = tile // CH
    slots = neighbours.shape[0]
    my_cells = lax.axis_index("cells")
    my_tm = lax.axis_index("tm")
    after = lax.rem(my_tm + 1, n_tm)
    before = lax.rem(my_tm + n_tm - 1, n_tm)
    has_left = my_cells > 0
    has_right = my_cells < n_cells - 1

    barrier = pltpu.get_barrier_semaphore()
    peers = [
        (lax.rem(my_tm + step // n_cells, n_tm), lax.rem(my_cells + step % n_cells, n_cells))
        for step in range(1, n_tm * n_cells)
    ]
    for peer_tm, peer_cells in peers:
        pl.semaphore_signal(
            barrier, inc=1, device_id={"tm": peer_tm, "cells": peer_cells}, device_id_type=MESH
        )
    groups = tile // (2 * CH)

    def loads(group):
        place = pl.ds(group * 2 * CH, 2 * CH)
        return (
            pltpu.make_async_copy(observed_hbm.at[:, place], observed.at[:, place], load_sem.at[0, group]),
            pltpu.make_async_copy(mask_hbm.at[:, place], mask.at[:, place], load_sem.at[1, group]),
        )

    order = (0, groups - 1) + tuple(range(1, groups - 1))
    for group in order:
        for load in loads(group):
            load.start()

    def to_cells(source, target, ssem, rsem, peer):
        return pltpu.make_async_remote_copy(
            src_ref=source, dst_ref=target, send_sem=ssem, recv_sem=rsem,
            device_id={"cells": peer}, device_id_type=MESH,
        )

    def to_tm(source, target, ssem, rsem, peer):
        return pltpu.make_async_remote_copy(
            src_ref=source, dst_ref=target, send_sem=ssem, recv_sem=rsem,
            device_id={"tm": peer}, device_id_type=MESH,
        )

    def cell_copies(buffer_s, buffer_r, ssem, rsem):
        leftward = to_cells(
            buffer_s.at[0], buffer_r.at[1], ssem.at[0], rsem.at[1], jnp.maximum(my_cells - 1, 0)
        )
        rightward = to_cells(
            buffer_s.at[1], buffer_r.at[0], ssem.at[1], rsem.at[0], jnp.minimum(my_cells + 1, n_cells - 1)
        )
        return leftward, rightward

    def start_cells(copies):
        @pl.when(has_left)
        def _():
            copies[0].start()

        @pl.when(has_right)
        def _():
            copies[1].start()

    def wait_cells(copies):
        @pl.when(has_left)
        def _():
            copies[0].wait_send()
            copies[1].wait_recv()

        @pl.when(has_right)
        def _():
            copies[1].wait_send()
            copies[0].wait_recv()

    lanes = lax.broadcasted_iota(jnp.int32, (days // 4, L), 1)

    def columns(chunk):
        return pl.ds(chunk * CH if isinstance(chunk, int) else pl.multiple_of(chunk * CH, CH), CH)

    def store_scaled(chunk, vector):
        high, low = split(vector * spread[:, columns(chunk)])
        start = L + chunk * CH
        place = pl.ds(start if isinstance(chunk, int) else pl.multiple_of(start, L), CH)
        scaled[:days, place] = high
        scaled[days:, place] = low

    def send_edges(level):
        quarter = days // 4
        left = basis[level, :, :L] * spread[:, :L]
        right = basis[level, :, tile - L :] * spread[:, tile - L :]
        for side, block in ((0, left), (1, right)):
            packed = None
            for q in range(4):
                part = block[q * quarter : (q + 1) * quarter]
                shift = (q * HB - (0 if side == 0 else L - HB)) % L
                part = pltpu.roll(part, shift, 1) if shift else part
                packed = part if packed is None else jnp.where(lanes >= q * HB, part, packed)
            cell_send[level, side] = packed
        copies = cell_copies(
            cell_send.at[level], cell_recv.at[level], cell_ssem.at[level], cell_rsem.at[level]
        )
        start_cells(copies)
        return copies

    def take_edges(level, copies):
        quarter = days // 4
        wait_cells(copies)
        for side, flag, base in ((0, has_left, 0), (1, has_right, L + tile)):

            @pl.when(flag)
            def _(side=side, base=base):
                packed = cell_recv[level, side]
                for q in range(4):
                    shift = ((L - HB if side == 0 else 0) - q * HB) % L
                    part = pltpu.roll(packed, shift, 1) if shift else packed
                    keep = lanes >= L - HB if side == 0 else lanes < HB
                    high, low = split(jnp.where(keep, part, 0.0))
                    scaled[q * quarter : (q + 1) * quarter, base : base + L] = high
                    scaled[days + q * quarter : days + (q + 1) * quarter, base : base + L] = low

    region_row[:, L : L + tile] = regions[...]

    eye = lax.broadcasted_iota(jnp.int32, (L, L), 0) == lax.broadcasted_iota(jnp.int32, (L, L), 1)
    ones = jnp.ones((L, L), BF16)

    def column_block(block):
        row = region_row[:, block * L : (block + 1) * L].astype(F32)
        diagonal = jnp.where(eye, row, 0.0).astype(BF16)
        column_ids[block * L : (block + 1) * L, :] = dot(diagonal, ones)

    span = L + 2 * HB
    span_ids = lax.broadcasted_iota(jnp.int32, (span, L), 0)

    def count_chunk(chunk):
        counts[chunk] = jnp.zeros((2 * CH, CH), BF16)
        for half in range(2):
            start = chunk * CH + half * L
            place = pl.ds(start, L)
            ids = span_ids + (my_cells * tile + start - HB)
            found = jnp.zeros((span, L), F32)
            for slot in range(slots):
                found = jnp.where(ids == neighbours[pl.ds(slot, 1), place], found + 1.0, found)
            same = column_ids[start + L - HB : start + L - HB + span, :] == regions[:, place].astype(F32)
            found = jnp.where(same, found, 0.0)
            counts[chunk, half * L + L - HB : half * L + L - HB + span, half * L : half * L + L] = found.astype(BF16)

    def build_toeplitz():
        rows_t = 2 * W
        gap = jnp.abs(
            lax.broadcasted_iota(jnp.int32, (rows_t, L), 0) + W - lax.broadcasted_iota(jnp.int32, (rows_t, L), 1)
        )
        band = jnp.zeros((rows_t, L), F32)
        for k in range(W):
            band = jnp.where(gap == k + 1, taps[k] * (TAP_TOTAL / W / TAU), band)
        wide = jnp.concatenate([band, jnp.zeros((rows_t, days - L), F32)], axis=1)
        lanes_t = lax.broadcasted_iota(jnp.int32, (rows_t, days), 1)
        for row in range(0, days, rows_t):
            shift = (row - W) % days
            near = pltpu.roll(wide, shift, 1) if shift else wide
            near = jnp.where((lanes_t >= row - W) & (lanes_t < row + rows_t + W), near, 0.0)
            high, low = split(near)
            toeplitz[row : row + rows_t] = jnp.concatenate([high, low, high], axis=1)
        for side, part in ((0, band[:W, :W]), (1, band[W:, L - W :])):
            high, low = split(part)
            edge_t[side] = jnp.concatenate([high, low, high], axis=1)

    for block in range(1, 1 + tile // L):
        column_block(block)

    middle = (tuple(range(2, chunks - 2)),)
    rest = ((1,), (chunks - 2,))
    ends = ((0,), (chunks - 1,))

    def count_runs(runs):
        for run in runs:
            for chunk in run:
                count_chunk(chunk)

    scaled[:, :L] = jnp.zeros((2 * days, L), BF16)
    scaled[:, L + tile :] = jnp.zeros((2 * days, L), BF16)

    def first_vector(group):
        for load in loads(group):
            load.wait()
        for chunk in (2 * group, 2 * group + 1):
            value = observed[:, columns(chunk)] * mask[:, columns(chunk)].astype(F32)
            basis[0, :, columns(chunk)] = value
            store_scaled(chunk, value)

    count_runs(middle)
    first_vector(0)
    first_vector(groups - 1)
    pl.semaphore_wait(barrier, n_tm * n_cells - 1)
    region_send[0] = jnp.broadcast_to(regions[:, :L], (8, L))
    region_send[1] = jnp.broadcast_to(regions[:, tile - L :], (8, L))
    region_copies = cell_copies(region_send, region_recv, region_ssem, region_rsem)
    start_cells(region_copies)
    copies = send_edges(0)
    for group in order[2:]:
        first_vector(group)

    moments[...] = jnp.zeros_like(moments)

    def fold(product):
        total = jnp.sum(product.reshape(days // 8, 8, CH), axis=0)
        return total[:, :L] + total[:, L:]

    def day_copies(level, run):
        place = pl.ds(run[0] * CH, len(run) * CH)
        return (
            to_tm(
                day_send.at[level, 0, :, place], day_recv.at[level, 1, :, place],
                day_ssem.at[level, 0, run[0]], day_rsem.at[level, 1, run[0]], before,
            ),
            to_tm(
                day_send.at[level, 1, :, place], day_recv.at[level, 0, :, place],
                day_ssem.at[level, 1, run[0]], day_rsem.at[level, 0, run[0]], after,
            ),
        )

    def gather(level, chunk):
        place = columns(chunk)
        window = pl.ds(chunk * CH, 2 * CH)
        both = jnp.concatenate([scaled[:days, window], scaled[days:, window]], axis=1)
        gathered = dot(both, jnp.concatenate([counts[chunk], counts[chunk]], axis=0))
        mixed = basis[level, :, place] + (PAIR * spread[:, place]) * gathered
        day_send[level, 0, :, place] = mixed[:W]
        day_send[level, 1, :, place] = mixed[days - W :]
        basis[level + 1, :, place] = mixed

    def smoothen(level, chunk):
        place = columns(chunk)
        mixed = basis[level + 1, :, place]
        high, low = split(mixed)
        basis[level + 1, :, place] = (DIAG / TAU) * mixed + dot(
            toeplitz[...], jnp.concatenate([high, high, low], axis=0)
        )

    def spatial(level, runs, between=None):
        for run in runs:
            for chunk in run:
                gather(level, chunk)
        for run in runs:
            for copy in day_copies(level, run):
                copy.start()
        if between is not None:
            between()
        for run in runs:
            for chunk in run:
                smoothen(level, chunk)

    def finish(level, runs):
        for run in runs:
            for copy in day_copies(level, run):
                copy.wait()
        for run in runs:
            for chunk in run:
                finish_chunk(level, chunk)

    def finish_chunk(level, chunk):
        place = columns(chunk)
        smooth = basis[level + 1, :, place]
        ends = []
        for side in range(2):
            high, low = split(day_recv[level, side, :, place])
            ends.append(dot(edge_t[side], jnp.concatenate([high, high, low], axis=0)))
        smooth = jnp.concatenate(
            [smooth[:W] + ends[0], smooth[W : days - W], smooth[days - W :] + ends[1]], axis=0
        )
        vector = basis[level, :, place]
        image = ((noise[:, place] - SHIFT) * (1.0 / TAU)) * vector + mask[:, place].astype(F32) * smooth
        if level == 1:
            start = basis[0, :, place]
            other = vector - lead[:, :CH] * start
            image = image - lead[:, :CH] * (vector + other)
            vector = other
            basis[1, :, place] = vector
        elif level == 2:
            image = image - lead[:, :CH] * vector
        basis[level + 1, :, place] = image
        moments[2 * level] += fold(vector * vector)
        moments[2 * level + 1] += fold(vector * image)
        if level + 1 < ITERS:
            store_scaled(chunk, image)

    row_ids = lax.broadcasted_iota(jnp.int32, (8, L), 0)

    def start_sum(source, gathered, ssem, rsem, me, count, send):
        gathered[me] = source[...]
        for step in range(1, count):
            peer = lax.rem(me + step, count)
            send(source, gathered.at[me], ssem.at[step], rsem.at[me], peer).start()

    def end_sum(source, gathered, ssem, rsem, me, count, send):
        for step in range(1, count):
            peer = lax.rem(me + step, count)
            send(source, gathered.at[peer], ssem.at[step], rsem.at[peer], peer).wait()
        total = gathered[0]
        for index in range(1, count):
            total = total + gathered[index]
        return total

    def over_tm(turn):
        return (partial.at[turn, 0], gather_tm.at[turn], tm_ssem.at[turn], tm_rsem.at[turn], my_tm, n_tm, to_tm)

    def over_cells(turn):
        return (
            partial.at[turn, 1], gather_cells.at[turn], cells_ssem.at[turn], cells_rsem.at[turn],
            my_cells, n_cells, to_cells,
        )

    def packed_moments(first, last):
        packed = jnp.zeros((8, L), F32)
        for k in range(first, last):
            packed = jnp.where(row_ids == k, jnp.sum(moments[k], axis=0, keepdims=True), packed)
        return packed

    def lane_sums(total, first, last):
        return [
            jnp.broadcast_to(jnp.sum(total[k : k + 1], axis=1, keepdims=True), (1, CH))
            for k in range(first, last)
        ]

    mine = my_cells * n_tm + my_tm

    def to_peer(peer_tm, peer_cells, step, slot):
        return pltpu.make_async_remote_copy(
            src_ref=gather_all.at[mine], dst_ref=gather_all.at[slot],
            send_sem=all_ssem.at[step], recv_sem=all_rsem.at[slot],
            device_id={"tm": peer_tm, "cells": peer_cells}, device_id_type=MESH,
        )

    def sums_begin(turn, first, last):
        partial[turn, 0] = packed_moments(first, last)
        start_sum(*over_tm(turn))

    def sums_middle(turn):
        partial[turn, 1] = end_sum(*over_tm(turn))
        start_sum(*over_cells(turn))

    def sums_end(turn, first, last):
        return lane_sums(end_sum(*over_cells(turn)), first, last)

    spatial(0, middle, build_toeplitz)
    count_runs(rest)
    spatial(0, rest)
    wait_cells(region_copies)
    region_row[:, :L] = jnp.where(has_left, region_recv[0, :1], -1)
    region_row[:, L + tile :] = jnp.where(has_right, region_recv[1, :1], -1)
    column_block(0)
    column_block(1 + tile // L)
    count_runs(ends)
    take_edges(0, copies)
    spatial(0, ends)

    for level in range(ITERS - 1):
        if level == 1:
            sums = sums_end(0, 0, 2)
            factor_now = sums[1] / sums[0]
            lead[...] = factor_now
            norm_first = sums[0]
        finish(level, middle)
        finish(level, rest)
        spatial(level + 1, middle)
        finish(level, ends)
        copies = send_edges(level + 1)
        if level == 0:
            sums_begin(0, 0, 2)
        spatial(level + 1, rest)
        if level == 0:
            sums_middle(0)
        take_edges(level + 1, copies)
        spatial(level + 1, ends)
    finish(ITERS - 1, middle)
    finish(ITERS - 1, rest)
    finish(ITERS - 1, ends)
    gather_all[mine] = packed_moments(2, 2 * ITERS)
    for step, (peer_tm, peer_cells) in enumerate(peers):
        to_peer(peer_tm, peer_cells, step, mine).start()
    rho = SHIFT + TAU * factor_now
    for step, (peer_tm, peer_cells) in enumerate(peers):
        to_peer(peer_tm, peer_cells, step, peer_cells * n_tm + peer_tm).wait()
    total = gather_all[0]
    for index in range(1, n_tm * n_cells):
        total = total + gather_all[index]
    tail = lane_sums(total, 2, 2 * ITERS)
    iterate, residual = polynomial_steps([norm_first, jnp.zeros_like(norm_first)] + tail, rho)

    def save(group):
        place = pl.ds(group * 2 * CH, 2 * CH)
        return (
            pltpu.make_async_copy(observed.at[:, place], solution_out.at[:, place], store_sem.at[0, group]),
            pltpu.make_async_copy(last_residual.at[:, place], residual_out.at[:, place], store_sem.at[1, group]),
        )

    for group in range(groups):
        for chunk in (2 * group, 2 * group + 1):
            place = columns(chunk)
            levels = [basis[k, :, place] for k in range(ITERS + 1)]
            observed[:, place] = combine(iterate, levels)
            last_residual[:, place] = combine(residual, levels)
        for copy in save(group):
            copy.start()
    for group in range(groups):
        for copy in save(group):
            copy.wait()


def on_device(n_cells, n_tm, observed, mask, noise, spread, taps, neighbours, regions):
    days, tile = observed.shape
    chunks = tile // CH
    dma = pltpu.SemaphoreType.DMA
    vmem = pl.BlockSpec(memory_space=pltpu.VMEM)
    return pl.pallas_call(
        functools.partial(kernel, n_cells, n_tm),
        out_shape=(pltpu.VMEM((days, tile), F32), pltpu.VMEM((days, tile), F32)),
        in_specs=[pl.BlockSpec(memory_space=pltpu.SMEM)] + [pl.BlockSpec(memory_space=pl.ANY)] * 2 + [vmem] * 4,
        out_specs=(pl.BlockSpec(memory_space=pl.ANY), pl.BlockSpec(memory_space=pl.ANY)),
        scratch_shapes=[
            pltpu.VMEM((days, tile), F32),
            pltpu.VMEM((days, tile), jnp.int32),
            pltpu.VMEM((days, tile), F32),
            pltpu.VMEM((ITERS + 1, days, tile), F32),
            pltpu.VMEM((2 * days, tile + 2 * L), BF16),
            pltpu.VMEM((chunks, 2 * CH, CH), BF16),
            pltpu.VMEM((days, 3 * days), BF16),
            pltpu.VMEM((2, W, 3 * W), BF16),
            pltpu.VMEM((tile + 2 * L, L), F32),
            pltpu.VMEM((1, tile + 2 * L), jnp.int32),
            pltpu.VMEM((2, 8, L), jnp.int32),
            pltpu.VMEM((2, 8, L), jnp.int32),
            pltpu.VMEM((ITERS, 2, W, tile), F32),
            pltpu.VMEM((ITERS, 2, W, tile), F32),
            pltpu.VMEM((ITERS, 2, days // 4, L), F32),
            pltpu.VMEM((ITERS, 2, days // 4, L), F32),
            pltpu.VMEM((1, 2, 8, L), F32),
            pltpu.VMEM((2 * ITERS, 8, L), F32),
            pltpu.VMEM((1, n_tm, 8, L), F32),
            pltpu.VMEM((1, n_cells, 8, L), F32),
            pltpu.VMEM((1, CH), F32),
            dma((ITERS, 2, chunks)),
            dma((ITERS, 2, chunks)),
            dma((ITERS, 2)),
            dma((ITERS, 2)),
            dma((2,)),
            dma((2,)),
            dma((1, n_tm)),
            dma((1, n_tm)),
            dma((1, n_cells)),
            dma((1, n_cells)),
            dma((2, chunks // 2)),
            dma((2, chunks // 2)),
            pltpu.VMEM((n_cells * n_tm, 8, L), F32),
            dma((n_cells * n_tm,)),
            dma((n_cells * n_tm,)),
        ],
        compiler_params=pltpu.CompilerParams(
            collective_id=0, has_side_effects=True, vmem_limit_bytes=52 * 1024 * 1024
        ),
    )(taps, observed, mask, noise[None, :], spread[None, :], neighbours, regions[None, :])


def solution(mesh):
    return jax.shard_map(
        functools.partial(on_device, mesh.shape["cells"], mesh.shape["tm"]),
        mesh=mesh,
        in_specs=(
            P("tm", ("groups", "cells")),
            P("tm", ("groups", "cells")),
            P(("groups", "cells")),
            P(("groups", "cells")),
            P(),
            P(None, ("groups", "cells")),
            P(("groups", "cells")),
        ),
        out_specs=(P("tm", ("groups", "cells")), P("tm", ("groups", "cells"))),
        check_vma=False,
    )
```

```python
import functools

import jax
import jax.numpy as jnp
from jax import lax
from jax.experimental import pallas as pl
from jax.experimental.pallas import tpu as pltpu
from jax.sharding import PartitionSpec as P

MESH = pl.DeviceIdType.MESH
W = 32
HB = 32
ITERS = 3
PAIR = 0.075
DIAG = 2.0
TAP_TOTAL = 0.9
SHIFT = 2.3
TAU = 4.0
L = 128
CH = 256
F32 = jnp.float32
BF16 = jnp.bfloat16


def split(values):
    high = values.astype(BF16)
    return high, (values - high.astype(F32)).astype(BF16)


def dot(a, b):
    return jnp.dot(a, b, preferred_element_type=F32)


def combine(factors, vectors):
    total = factors[0] * vectors[0]
    for factor, vector in zip(factors[1:], vectors[1:]):
        total = total + factor * vector
    return total


def polynomial_steps(moments, rho):
    def form(left, right, up):
        total = None
        for i, a in enumerate(left):
            for j, b in enumerate(right):
                term = a * b * moments[i + j + up]
                total = term if total is None else total + term
        return total

    zero = jnp.zeros_like(moments[0])
    residual = [zero + 1.0]
    direction = [zero + 1.0]
    iterate = [zero] * ITERS
    norm_now = moments[0]
    for count in range(ITERS):
        alpha = norm_now / (rho * form(direction, direction, 0) + TAU * form(direction, direction, 1))
        image = [zero] * (len(direction) + 1)
        for k, value in enumerate(direction):
            image[k] = image[k] + rho * value
            image[k + 1] = image[k + 1] + TAU * value
            iterate[k] = iterate[k] + alpha * value
        residual = residual + [zero] * (len(image) - len(residual))
        residual = [r - alpha * q for r, q in zip(residual, image)]
        if count + 1 < ITERS:
            norm_next = form(residual, residual, 0)
            beta = norm_next / norm_now
            padded = direction + [zero] * (len(residual) - len(direction))
            direction = [r + beta * d for r, d in zip(residual, padded)]
            norm_now = norm_next
    return iterate, residual


def kernel(
    n_cells, n_tm,
    taps, observed_hbm, mask_hbm, noise, spread, neighbours, regions,
    solution_out, residual_out,
    observed, mask, last_residual, basis, scaled, counts, toeplitz, edge_t, column_ids, region_row, region_send, region_recv,
    day_send, day_recv, cell_send, cell_recv, partial, moments, gather_tm, gather_cells, lead,
    day_ssem, day_rsem, cell_ssem, cell_rsem, region_ssem, region_rsem,
    tm_ssem, tm_rsem, cells_ssem, cells_rsem, load_sem, store_sem,
):
    days, tile = observed.shape
    chunks = tile // CH
    slots = neighbours.shape[0]
    my_cells = lax.axis_index("cells")
    my_tm = lax.axis_index("tm")
    after = lax.rem(my_tm + 1, n_tm)
    before = lax.rem(my_tm + n_tm - 1, n_tm)
    has_left = my_cells > 0
    has_right = my_cells < n_cells - 1

    barrier = pltpu.get_barrier_semaphore()
    for step in range(1, n_tm):
        pl.semaphore_signal(
            barrier, inc=1, device_id={"tm": lax.rem(my_tm + step, n_tm)}, device_id_type=MESH
        )
    for step in range(1, n_cells):
        pl.semaphore_signal(
            barrier, inc=1, device_id={"cells": lax.rem(my_cells + step, n_cells)}, device_id_type=MESH
        )
    groups = tile // (2 * CH)

    def loads(group):
        place = pl.ds(group * 2 * CH, 2 * CH)
        return (
            pltpu.make_async_copy(observed_hbm.at[:, place], observed.at[:, place], load_sem.at[0, group]),
            pltpu.make_async_copy(mask_hbm.at[:, place], mask.at[:, place], load_sem.at[1, group]),
        )

    order = (0, groups - 1) + tuple(range(1, groups - 1))
    for group in order:
        for load in loads(group):
            load.start()

    def to_cells(source, target, ssem, rsem, peer):
        return pltpu.make_async_remote_copy(
            src_ref=source, dst_ref=target, send_sem=ssem, recv_sem=rsem,
            device_id={"cells": peer}, device_id_type=MESH,
        )

    def to_tm(source, target, ssem, rsem, peer):
        return pltpu.make_async_remote_copy(
            src_ref=source, dst_ref=target, send_sem=ssem, recv_sem=rsem,
            device_id={"tm": peer}, device_id_type=MESH,
        )

    def cell_copies(buffer_s, buffer_r, ssem, rsem):
        leftward = to_cells(
            buffer_s.at[0], buffer_r.at[1], ssem.at[0], rsem.at[1], jnp.maximum(my_cells - 1, 0)
        )
        rightward = to_cells(
            buffer_s.at[1], buffer_r.at[0], ssem.at[1], rsem.at[0], jnp.minimum(my_cells + 1, n_cells - 1)
        )
        return leftward, rightward

    def start_cells(copies):
        @pl.when(has_left)
        def _():
            copies[0].start()

        @pl.when(has_right)
        def _():
            copies[1].start()

    def wait_cells(copies):
        @pl.when(has_left)
        def _():
            copies[0].wait_send()
            copies[1].wait_recv()

        @pl.when(has_right)
        def _():
            copies[1].wait_send()
            copies[0].wait_recv()

    lanes = lax.broadcasted_iota(jnp.int32, (days // 4, L), 1)

    def columns(chunk):
        return pl.ds(chunk * CH if isinstance(chunk, int) else pl.multiple_of(chunk * CH, CH), CH)

    def store_scaled(chunk, vector):
        high, low = split(vector * spread[:, columns(chunk)])
        start = L + chunk * CH
        place = pl.ds(start if isinstance(chunk, int) else pl.multiple_of(start, L), CH)
        scaled[:days, place] = high
        scaled[days:, place] = low

    def send_edges(level):
        quarter = days // 4
        left = basis[level, :, :L] * spread[:, :L]
        right = basis[level, :, tile - L :] * spread[:, tile - L :]
        for side, block in ((0, left), (1, right)):
            packed = None
            for q in range(4):
                part = block[q * quarter : (q + 1) * quarter]
                shift = (q * HB - (0 if side == 0 else L - HB)) % L
                part = pltpu.roll(part, shift, 1) if shift else part
                packed = part if packed is None else jnp.where(lanes >= q * HB, part, packed)
            cell_send[level, side] = packed
        copies = cell_copies(
            cell_send.at[level], cell_recv.at[level], cell_ssem.at[level], cell_rsem.at[level]
        )
        start_cells(copies)
        return copies

    def take_edges(level, copies):
        quarter = days // 4
        wait_cells(copies)
        for side, flag, base in ((0, has_left, 0), (1, has_right, L + tile)):

            @pl.when(flag)
            def _(side=side, base=base):
                packed = cell_recv[level, side]
                for q in range(4):
                    shift = ((L - HB if side == 0 else 0) - q * HB) % L
                    part = pltpu.roll(packed, shift, 1) if shift else packed
                    keep = lanes >= L - HB if side == 0 else lanes < HB
                    high, low = split(jnp.where(keep, part, 0.0))
                    scaled[q * quarter : (q + 1) * quarter, base : base + L] = high
                    scaled[days + q * quarter : days + (q + 1) * quarter, base : base + L] = low

    region_row[:, L : L + tile] = regions[...]

    eye = lax.broadcasted_iota(jnp.int32, (L, L), 0) == lax.broadcasted_iota(jnp.int32, (L, L), 1)
    ones = jnp.ones((L, L), BF16)

    def column_block(block):
        row = region_row[:, block * L : (block + 1) * L].astype(F32)
        diagonal = jnp.where(eye, row, 0.0).astype(BF16)
        column_ids[block * L : (block + 1) * L, :] = dot(diagonal, ones)

    span = L + 2 * HB
    span_ids = lax.broadcasted_iota(jnp.int32, (span, L), 0)

    def count_chunk(chunk):
        counts[chunk] = jnp.zeros((2 * CH, CH), BF16)
        for half in range(2):
            start = chunk * CH + half * L
            place = pl.ds(start, L)
            ids = span_ids + (my_cells * tile + start - HB)
            found = jnp.zeros((span, L), F32)
            for slot in range(slots):
                found = jnp.where(ids == neighbours[pl.ds(slot, 1), place], found + 1.0, found)
            same = column_ids[start + L - HB : start + L - HB + span, :] == regions[:, place].astype(F32)
            found = jnp.where(same, found, 0.0)
            counts[chunk, half * L + L - HB : half * L + L - HB + span, half * L : half * L + L] = found.astype(BF16)

    def build_toeplitz():
        rows_t = 2 * W
        gap = jnp.abs(
            lax.broadcasted_iota(jnp.int32, (rows_t, L), 0) + W - lax.broadcasted_iota(jnp.int32, (rows_t, L), 1)
        )
        band = jnp.zeros((rows_t, L), F32)
        for k in range(W):
            band = jnp.where(gap == k + 1, taps[k] * (TAP_TOTAL / W / TAU), band)
        wide = jnp.concatenate([band, jnp.zeros((rows_t, days - L), F32)], axis=1)
        lanes_t = lax.broadcasted_iota(jnp.int32, (rows_t, days), 1)
        for row in range(0, days, rows_t):
            shift = (row - W) % days
            near = pltpu.roll(wide, shift, 1) if shift else wide
            near = jnp.where((lanes_t >= row - W) & (lanes_t < row + rows_t + W), near, 0.0)
            high, low = split(near)
            toeplitz[row : row + rows_t] = jnp.concatenate([high, low, high], axis=1)
        for side, part in ((0, band[:W, :W]), (1, band[W:, L - W :])):
            high, low = split(part)
            edge_t[side] = jnp.concatenate([high, low, high], axis=1)

    for block in range(1, 1 + tile // L):
        column_block(block)

    middle = (tuple(range(3, chunks - 3)), (2,), (chunks - 3,))
    rest = ((1,), (chunks - 2,))
    ends = ((0,), (chunks - 1,))

    def count_runs(runs):
        for run in runs:
            for chunk in run:
                count_chunk(chunk)

    scaled[:, :L] = jnp.zeros((2 * days, L), BF16)
    scaled[:, L + tile :] = jnp.zeros((2 * days, L), BF16)

    def first_vector(group):
        for load in loads(group):
            load.wait()
        for chunk in (2 * group, 2 * group + 1):
            value = observed[:, columns(chunk)] * mask[:, columns(chunk)].astype(F32)
            basis[0, :, columns(chunk)] = value
            store_scaled(chunk, value)

    count_runs(middle)
    first_vector(0)
    first_vector(groups - 1)
    pl.semaphore_wait(barrier, n_tm + n_cells - 2)
    region_send[0] = jnp.broadcast_to(regions[:, :L], (8, L))
    region_send[1] = jnp.broadcast_to(regions[:, tile - L :], (8, L))
    region_copies = cell_copies(region_send, region_recv, region_ssem, region_rsem)
    start_cells(region_copies)
    copies = send_edges(0)
    for group in order[2:]:
        first_vector(group)

    moments[...] = jnp.zeros_like(moments)

    def fold(product):
        total = jnp.sum(product.reshape(days // 8, 8, CH), axis=0)
        return total[:, :L] + total[:, L:]

    def day_copies(level, run):
        place = pl.ds(run[0] * CH, len(run) * CH)
        return (
            to_tm(
                day_send.at[level, 0, :, place], day_recv.at[level, 1, :, place],
                day_ssem.at[level, 0, run[0]], day_rsem.at[level, 1, run[0]], before,
            ),
            to_tm(
                day_send.at[level, 1, :, place], day_recv.at[level, 0, :, place],
                day_ssem.at[level, 1, run[0]], day_rsem.at[level, 0, run[0]], after,
            ),
        )

    def gather(level, chunk):
        place = columns(chunk)
        window = pl.ds(chunk * CH, 2 * CH)
        both = jnp.concatenate([scaled[:days, window], scaled[days:, window]], axis=1)
        gathered = dot(both, jnp.concatenate([counts[chunk], counts[chunk]], axis=0))
        mixed = basis[level, :, place] + (PAIR * spread[:, place]) * gathered
        day_send[level, 0, :, place] = mixed[:W]
        day_send[level, 1, :, place] = mixed[days - W :]
        basis[level + 1, :, place] = mixed

    def smoothen(level, chunk):
        place = columns(chunk)
        mixed = basis[level + 1, :, place]
        high, low = split(mixed)
        basis[level + 1, :, place] = (DIAG / TAU) * mixed + dot(
            toeplitz[...], jnp.concatenate([high, high, low], axis=0)
        )

    def spatial(level, runs, between=None):
        for run in runs:
            for chunk in run:
                gather(level, chunk)
        for run in runs:
            for copy in day_copies(level, run):
                copy.start()
        if between is not None:
            between()
        for run in runs:
            for chunk in run:
                smoothen(level, chunk)

    def finish(level, runs):
        for run in runs:
            for copy in day_copies(level, run):
                copy.wait()
        for run in runs:
            for chunk in run:
                finish_chunk(level, chunk)

    def finish_chunk(level, chunk):
        place = columns(chunk)
        smooth = basis[level + 1, :, place]
        ends = []
        for side in range(2):
            high, low = split(day_recv[level, side, :, place])
            ends.append(dot(edge_t[side], jnp.concatenate([high, high, low], axis=0)))
        smooth = jnp.concatenate(
            [smooth[:W] + ends[0], smooth[W : days - W], smooth[days - W :] + ends[1]], axis=0
        )
        vector = basis[level, :, place]
        image = ((noise[:, place] - SHIFT) * (1.0 / TAU)) * vector + mask[:, place].astype(F32) * smooth
        if level == 1:
            start = basis[0, :, place]
            other = vector - lead[:, :CH] * start
            image = image - lead[:, :CH] * (vector + other)
            vector = other
            basis[1, :, place] = vector
        elif level == 2:
            image = image - lead[:, :CH] * vector
        basis[level + 1, :, place] = image
        moments[2 * level] += fold(vector * vector)
        moments[2 * level + 1] += fold(vector * image)
        if level + 1 < ITERS:
            store_scaled(chunk, image)

    row_ids = lax.broadcasted_iota(jnp.int32, (8, L), 0)

    def start_sum(source, gathered, ssem, rsem, me, count, send):
        gathered[me] = source[...]
        for step in range(1, count):
            peer = lax.rem(me + step, count)
            send(source, gathered.at[me], ssem.at[step], rsem.at[me], peer).start()

    def end_sum(source, gathered, ssem, rsem, me, count, send):
        for step in range(1, count):
            peer = lax.rem(me + step, count)
            send(source, gathered.at[peer], ssem.at[step], rsem.at[peer], peer).wait()
        total = gathered[0]
        for index in range(1, count):
            total = total + gathered[index]
        return total

    def over_tm(turn):
        return (partial.at[turn, 0], gather_tm.at[turn], tm_ssem.at[turn], tm_rsem.at[turn], my_tm, n_tm, to_tm)

    def over_cells(turn):
        return (
            partial.at[turn, 1], gather_cells.at[turn], cells_ssem.at[turn], cells_rsem.at[turn],
            my_cells, n_cells, to_cells,
        )

    def packed_moments(first, last):
        packed = jnp.zeros((8, L), F32)
        for k in range(first, last):
            packed = jnp.where(row_ids == k, jnp.sum(moments[k], axis=0, keepdims=True), packed)
        return packed

    def lane_sums(total, first, last):
        return [
            jnp.broadcast_to(jnp.sum(total[k : k + 1], axis=1, keepdims=True), (1, CH))
            for k in range(first, last)
        ]

    def sums_begin(turn, first, last):
        partial[turn, 0] = packed_moments(first, last)
        start_sum(*over_tm(turn))

    def sums_middle(turn):
        partial[turn, 1] = end_sum(*over_tm(turn))
        start_sum(*over_cells(turn))

    def sums_end(turn, first, last):
        return lane_sums(end_sum(*over_cells(turn)), first, last)

    spatial(0, middle[:1], build_toeplitz)
    spatial(0, middle[1:])
    count_runs(rest)
    spatial(0, rest)
    wait_cells(region_copies)
    region_row[:, :L] = jnp.where(has_left, region_recv[0, :1], -1)
    region_row[:, L + tile :] = jnp.where(has_right, region_recv[1, :1], -1)
    column_block(0)
    column_block(1 + tile // L)
    count_runs(ends)
    take_edges(0, copies)
    spatial(0, ends)

    for level in range(ITERS - 1):
        if level == 1:
            sums = sums_end(0, 0, 2)
            factor_now = sums[1] / sums[0]
            lead[...] = factor_now
            norm_first = sums[0]
        finish(level, middle)
        finish(level, rest)
        spatial(level + 1, middle)
        finish(level, ends)
        copies = send_edges(level + 1)
        if level == 0:
            sums_begin(0, 0, 2)
        spatial(level + 1, rest)
        if level == 0:
            sums_middle(0)
        take_edges(level + 1, copies)
        spatial(level + 1, ends)
    finish(ITERS - 1, middle)
    finish(ITERS - 1, rest)
    finish(ITERS - 1, ends)
    sums_begin(1, 2, 2 * ITERS)
    sums_middle(1)
    rho = SHIFT + TAU * factor_now
    tail = sums_end(1, 2, 2 * ITERS)
    iterate, residual = polynomial_steps([norm_first, jnp.zeros_like(norm_first)] + tail, rho)

    def save(group):
        place = pl.ds(group * 2 * CH, 2 * CH)
        return (
            pltpu.make_async_copy(observed.at[:, place], solution_out.at[:, place], store_sem.at[0, group]),
            pltpu.make_async_copy(last_residual.at[:, place], residual_out.at[:, place], store_sem.at[1, group]),
        )

    for group in range(groups):
        for chunk in (2 * group, 2 * group + 1):
            place = columns(chunk)
            levels = [basis[k, :, place] for k in range(ITERS + 1)]
            observed[:, place] = combine(iterate, levels)
            last_residual[:, place] = combine(residual, levels)
        for copy in save(group):
            copy.start()
    for group in range(groups):
        for copy in save(group):
            copy.wait()


def on_device(n_cells, n_tm, observed, mask, noise, spread, taps, neighbours, regions):
    days, tile = observed.shape
    chunks = tile // CH
    dma = pltpu.SemaphoreType.DMA
    vmem = pl.BlockSpec(memory_space=pltpu.VMEM)
    return pl.pallas_call(
        functools.partial(kernel, n_cells, n_tm),
        out_shape=(pltpu.VMEM((days, tile), F32), pltpu.VMEM((days, tile), F32)),
        in_specs=[pl.BlockSpec(memory_space=pltpu.SMEM)] + [pl.BlockSpec(memory_space=pl.ANY)] * 2 + [vmem] * 4,
        out_specs=(pl.BlockSpec(memory_space=pl.ANY), pl.BlockSpec(memory_space=pl.ANY)),
        scratch_shapes=[
            pltpu.VMEM((days, tile), F32),
            pltpu.VMEM((days, tile), jnp.int32),
            pltpu.VMEM((days, tile), F32),
            pltpu.VMEM((ITERS + 1, days, tile), F32),
            pltpu.VMEM((2 * days, tile + 2 * L), BF16),
            pltpu.VMEM((chunks, 2 * CH, CH), BF16),
            pltpu.VMEM((days, 3 * days), BF16),
            pltpu.VMEM((2, W, 3 * W), BF16),
            pltpu.VMEM((tile + 2 * L, L), F32),
            pltpu.VMEM((1, tile + 2 * L), jnp.int32),
            pltpu.VMEM((2, 8, L), jnp.int32),
            pltpu.VMEM((2, 8, L), jnp.int32),
            pltpu.VMEM((ITERS, 2, W, tile), F32),
            pltpu.VMEM((ITERS, 2, W, tile), F32),
            pltpu.VMEM((ITERS, 2, days // 4, L), F32),
            pltpu.VMEM((ITERS, 2, days // 4, L), F32),
            pltpu.VMEM((2, 2, 8, L), F32),
            pltpu.VMEM((2 * ITERS, 8, L), F32),
            pltpu.VMEM((2, n_tm, 8, L), F32),
            pltpu.VMEM((2, n_cells, 8, L), F32),
            pltpu.VMEM((1, CH), F32),
            dma((ITERS, 2, chunks)),
            dma((ITERS, 2, chunks)),
            dma((ITERS, 2)),
            dma((ITERS, 2)),
            dma((2,)),
            dma((2,)),
            dma((2, n_tm)),
            dma((2, n_tm)),
            dma((2, n_cells)),
            dma((2, n_cells)),
            dma((2, chunks // 2)),
            dma((2, chunks // 2)),
        ],
        compiler_params=pltpu.CompilerParams(
            collective_id=0, has_side_effects=True, vmem_limit_bytes=52 * 1024 * 1024
        ),
    )(taps, observed, mask, noise[None, :], spread[None, :], neighbours, regions[None, :])


def solution(mesh):
    return jax.shard_map(
        functools.partial(on_device, mesh.shape["cells"], mesh.shape["tm"]),
        mesh=mesh,
        in_specs=(
            P("tm", ("groups", "cells")),
            P("tm", ("groups", "cells")),
            P(("groups", "cells")),
            P(("groups", "cells")),
            P(),
            P(None, ("groups", "cells")),
            P(("groups", "cells")),
        ),
        out_specs=(P("tm", ("groups", "cells")), P("tm", ("groups", "cells"))),
        check_vma=False,
    )
```
